32 devices in a mesh: groups: 2 (over y), tensor: 4 (over x, core), batch: 4 (over z).
Axes of the slice: x: 2, y: 2, z: 4, core: 2. Of those that a mesh axis runs over, the one named last changes fastest.
Arguments:
- tokens: bfloat16 [64, 3, 4096], P(('groups', 'batch')), parts along dimension 0, may hold values from -200 to 200
- q_weight: bfloat16 [4096, 8192], P(None, 'tensor'), may hold values from -0.09375 to 0.09375
- kv_weight: bfloat16 [4096, 2048], P(None, 'tensor'), may hold values from -2 to 2
- old_keys: bfloat16 [4, 96, 512, 512], P('tensor', ('groups', 'batch')), parts along dimension 1, may hold values from -360 to 360
- old_values: bfloat16 [4, 96, 512, 512], P('tensor', ('groups', 'batch')), parts along dimension 1, may hold values from -18 to 18
- lengths: int32 [16, 4], P(('groups', 'batch')), parts along dimension 0, may hold values from 1 to 6, 12 in all within a row
- block_owner: int32 [16, 12], P(('groups', 'batch')), parts along dimension 0, may hold values from 0 to 3, as said below
Outputs:
- context: bfloat16 [64, 3, 8192], P(('groups', 'batch'), None, 'tensor'), parts along dimension 0
- new_keys: bfloat16 [8, 32, 512, 1024], P(('groups', 'batch'), 'tensor'), parts along dimension 0
- new_values: bfloat16 [8, 32, 512, 1024], P(('groups', 'batch'), 'tensor'), parts along dimension 0
The draws below stay inside these ranges and needn't reach their ends.
There are 2 independent parts, one for each index of `groups`. The reference program is written for one: setup_inputs(seed, part) draws one part's arguments, and reference() takes and returns one part's arrays. A program takes and returns all parts, laid end to end along the dimension named above; an argument that names none is the same for every part. Nothing has to cross between parts.
Inputs may be any that keep to these rules, and one draw needn't show every extreme that they name: `block_owner`: for every b, at most 8 of the 24 entries of rows 2 b and 2 b + 1 name the same index, and in every b some index is named by exactly 8 entries of row 2 b.
All inputs are finite; a program needn't handle non-finite values.
Results may differ from the reference program's by a relative error of at most 0.0065.
The reference program's roundings to bfloat16 on the way count: a program that leaves them out, or rounds other values in their place, can miss the bound.
Values may be sent and summed in bfloat16 or wider, within the bound.
No kernel may reach another device: no remote copies, remote signals or barrier semaphores. Data moves between devices by JAX's collectives and lax.ppermute only.
A program may use at most 256 MiB of HBM per device.

```python
import math
import jax
import jax.numpy as jnp
import numpy as np
from jax import lax

D = 4096
QH = 64
KV = 8
HD = 128
BLK = 512
STEPS = 3
REQ_OLD = 4
OLD_BLOCKS = 12
MAXB = 6
KV_OLD = 4
NEW_SLOTS = 8
REQUESTS = 32
N_TENSOR = 4
N_BATCH = 4


def draw_tokens(key, part):
    key = jax.random.fold_in(key, 11)
    base_key, column_key, row_key = jax.random.split(key, 3)
    base = jax.random.normal(base_key, (REQUESTS, STEPS, D), jnp.float32)
    columns = jnp.exp(jax.random.uniform(column_key, (1, 1, D), jnp.float32, 0.0, math.log(10.0)))
    row_scale = jnp.exp(jax.random.uniform(row_key, (REQUESTS, STEPS, 1), jnp.float32, math.log(0.3), math.log(3.0)))
    return jnp.clip(base * columns * row_scale, -200.0, 200.0).astype(jnp.bfloat16)


def draw_kv_weight(key, part):
    key = jax.random.fold_in(key, 41)
    base_key, factor_key = jax.random.split(key, 2)
    shape = (D, 2 * KV * HD)
    base = jax.random.normal(base_key, shape, jnp.float32)
    key_low = 3.0
    key_high = 12.0
    level = jax.random.uniform(factor_key, (1, 2 * KV * HD), jnp.float32)
    column = jnp.arange(2 * KV * HD)[None, :]
    key_factor = key_low * jnp.exp(level * math.log(key_high / key_low))
    value_factor = jnp.exp(level * math.log(3.0))
    factor = jnp.where(column < KV * HD, key_factor, value_factor)
    values = jnp.clip(base * factor / math.sqrt(D), -2.0, 2.0)
    return values.astype(jnp.bfloat16)


def draw_old_keys(key, part):
    key = jax.random.fold_in(key, 23)
    base_key = jax.random.fold_in(key, 0)
    shape = (N_TENSOR, N_BATCH * OLD_BLOCKS, BLK, KV_OLD * HD)
    base = jax.random.normal(base_key, shape, jnp.float32)
    values = jnp.clip(base * 2.0, -12.0, 12.0)
    return values.astype(jnp.bfloat16)


def draw_block_owner(key, part):
    key = jax.random.fold_in(key, 37)
    slots_device = 8 * OLD_BLOCKS // (3 * N_TENSOR)
    slot_total = N_TENSOR * slots_device

    def one_row(row_key):
        order_key, chosen_key, first_key, second_key = jax.random.split(row_key, 4)
        ordering = jax.random.permutation(order_key, slot_total).astype(jnp.int32)
        chosen = jax.random.randint(chosen_key, (), 0, N_TENSOR)
        slot_device = (jnp.arange(slot_total) // slots_device).astype(jnp.int32)
        scores = jnp.where(slot_device == chosen, jnp.arange(slot_total).astype(jnp.int32) - slot_total, ordering)
        ranked = jnp.argsort(scores, stable=True)
        devices = slot_device[ranked]
        first_perm = jax.random.permutation(first_key, OLD_BLOCKS)
        second_perm = jax.random.permutation(second_key, OLD_BLOCKS)
        first_row = jnp.zeros((OLD_BLOCKS,), jnp.int32).at[first_perm].set(devices[:OLD_BLOCKS])
        second_row = jnp.zeros((OLD_BLOCKS,), jnp.int32).at[second_perm].set(devices[OLD_BLOCKS:2 * OLD_BLOCKS])
        return jnp.stack([first_row, second_row])
    rows_all = jax.vmap(one_row)(jax.random.split(key, N_BATCH))
    return rows_all.reshape(2 * N_BATCH, OLD_BLOCKS).astype(jnp.int32)


def block_levels(key, shape, cuts, low, top_value):
    factor_of, own = 1.0, jax.random.fold_in(key, 6)
    for axis_at, blocks in cuts:
        heights = jnp.exp(jax.random.uniform(jax.random.fold_in(own, axis_at), (blocks,), jnp.float32, low / len(cuts), top_value / len(cuts)))
        factor_of = factor_of * jnp.repeat(heights, shape[axis_at] // blocks).reshape([-1 if axis == axis_at else 1 for axis in range(len(shape))])
    return factor_of


def split_up(number_of, total, reach, slope):
    weights = [(1 << 20) // math.isqrt(grade ** slope) + 1 for grade in range(2, number_of + 1)]
    spare, counts = total - reach - (number_of - 1), [1] * (number_of - 1)
    while spare > 0:
        free = [i for i in range(number_of - 1) if counts[i] < reach]
        mass, remaining = sum([weights[i] for i in free]), spare
        for i in free:
            addition = min(reach - counts[i], max(1, remaining * weights[i] // mass), spare)
            counts[i] = counts[i] + addition
            spare = spare - addition
    return np.array([reach] + counts)


def ragged(key, number_of, total, most, skew):
    if number_of == 2:
        one = jax.random.randint(key, (), max(1, total - most), min(most, total - 1) + 1)
        return jnp.stack([one, total - one])
    sizes = jnp.asarray(split_up(number_of, total, most, skew), jnp.int32)
    twos = (number_of - 1) // 2
    source_of, sink = sizes[1:1 + 2 * twos:2], sizes[2:2 + 2 * twos:2]
    margin = jnp.minimum(source_of - 1, most - sink)
    moved = jax.random.randint(jax.random.fold_in(key, 1), (twos,), 0, 1 << 20) % (margin + 1)
    sizes = sizes.at[1:1 + 2 * twos:2].set(source_of - moved).at[2:2 + 2 * twos:2].set(sink + moved)
    return sizes[jax.random.permutation(jax.random.fold_in(key, 2), number_of)]


def bell_draw(own_key, shape, deviation, reach, cuts=(), kind=jnp.bfloat16):
    drawn = deviation * jax.random.normal(own_key, shape, jnp.float32)
    if cuts:
        drawn = drawn * block_levels(own_key, shape, cuts, -0.22, 0.18)
    return jnp.clip(drawn, -reach, reach).astype(kind)


def setup_inputs(seed: int = 0, part: int = 0) -> dict:
    streams_of = jax.random.split(jax.random.key(seed), 8)
    own_keys = jax.random.split(jax.random.fold_in(streams_of[7], part), 8)
    tokens = draw_tokens(jax.random.fold_in(jax.random.fold_in(streams_of[7], part), 71), part)
    q_weight = bell_draw(streams_of[1], (D, QH * HD), D ** -0.5, 0.09375, ((1, 4),))
    kv_weight = draw_kv_weight(jax.random.fold_in(streams_of[7], 71), part)
    old_keys = draw_old_keys(jax.random.fold_in(jax.random.fold_in(streams_of[7], part), 71), part)
    old_values = bell_draw(own_keys[4], (N_TENSOR, N_BATCH * OLD_BLOCKS, BLK, KV_OLD * HD), 3.0, 18.0, ((0, 4), (1, 4)))
    lengths = jax.vmap(lambda own: ragged(own, REQ_OLD, OLD_BLOCKS, MAXB, 2))(jax.random.split(own_keys[5], (2 * N_BATCH))).reshape((2 * N_BATCH, REQ_OLD)).astype(jnp.int32)
    block_owner = draw_block_owner(jax.random.fold_in(jax.random.fold_in(streams_of[7], part), 71), part)
    return dict(tokens=tokens, q_weight=q_weight, kv_weight=kv_weight, old_keys=old_keys, old_values=old_values, lengths=lengths, block_owner=block_owner)


theta_base = 1000000.0
eps_norm = 1e-06
masked_low = -1e+30

def rotate(vectors, positions):
    half_dim = vectors.shape[-1] // 2
    frequency = theta_base ** (-2.0 * jnp.arange(half_dim, dtype=jnp.float32) / vectors.shape[-1])
    angles = positions[..., None, None] * frequency
    cosine = jnp.cos(angles)
    sine_part = jnp.sin(angles)
    lower_half = vectors[..., :half_dim]
    upper_half = vectors[..., half_dim:]
    return jnp.concatenate([lower_half * cosine - upper_half * sine_part, upper_half * cosine + lower_half * sine_part], axis=-1)

def block_requests(length_row, block_count):
    ends = jnp.cumsum(length_row)
    return lax.optimization_barrier(jnp.sum((jnp.arange(block_count)[:, None] >= ends[None, :]).astype(jnp.int32), axis=1))

def regroup(pool):
    old_width = N_TENSOR // 2
    kv_local = 2 * KV // N_TENSOR
    shaped = pool.reshape(2, old_width, N_BATCH, OLD_BLOCKS, BLK, kv_local * HD)
    shaped = jnp.transpose(shaped, (2, 0, 3, 4, 1, 5))
    return shaped.reshape(2 * N_BATCH, OLD_BLOCKS, BLK, KV * HD)

def migrate(pool, block_owner):
    blocks = regroup(pool).reshape(N_BATCH, 2 * OLD_BLOCKS, BLK, KV * HD)
    owners = block_owner.reshape(N_BATCH, 2 * OLD_BLOCKS)
    ordering = jnp.arange(2 * OLD_BLOCKS)
    same_owner = owners[:, :, None] == owners[:, None, :]
    block_rank = lax.optimization_barrier(jnp.sum((same_owner & (ordering[None, :, None] > ordering[None, None, :])).astype(jnp.int32), axis=2))
    slot_index = owners * NEW_SLOTS + block_rank + (jnp.arange(N_BATCH) * (N_TENSOR * NEW_SLOTS))[:, None]
    result = jnp.zeros((N_BATCH * N_TENSOR * NEW_SLOTS, BLK, KV * HD), pool.dtype)
    result = result.at[slot_index.reshape(-1)].set(blocks.reshape(-1, BLK, KV * HD))
    return result.reshape(N_BATCH, N_TENSOR * NEW_SLOTS, BLK, KV * HD)

def reference(tokens, q_weight, kv_weight, old_keys, old_values, lengths, block_owner):
    group_ratio = QH // KV
    score_scale = HD ** (-0.5)
    group_count = 2 * N_BATCH
    widened = tokens.astype(jnp.float32)
    normed = (widened * lax.rsqrt(lax.optimization_barrier(jnp.mean(widened * widened, axis=-1, keepdims=True)) + eps_norm)).astype(jnp.bfloat16)
    flattened = normed.reshape(REQUESTS * STEPS, D)
    query_rows = jnp.dot(flattened, q_weight, preferred_element_type=jnp.float32).astype(jnp.bfloat16)
    pair_rows = jnp.dot(flattened, kv_weight, preferred_element_type=jnp.float32).astype(jnp.bfloat16)
    starts = (lengths.reshape(-1) * BLK).astype(jnp.float32)
    positions = starts[:, None] + jnp.arange(STEPS, dtype=jnp.float32)[None, :]
    queries = rotate(query_rows.astype(jnp.float32).reshape(REQUESTS, STEPS, QH, HD), positions).astype(jnp.bfloat16)
    fresh_keys = rotate(pair_rows[:, :KV * HD].astype(jnp.float32).reshape(REQUESTS, STEPS, KV, HD), positions).astype(jnp.bfloat16)
    fresh_values = pair_rows[:, KV * HD:].reshape(REQUESTS, STEPS, KV, HD)
    key_blocks = regroup(old_keys).reshape(group_count, OLD_BLOCKS, BLK, KV, HD)
    value_blocks = regroup(old_values).reshape(group_count, OLD_BLOCKS, BLK, KV, HD)
    causal = jnp.arange(STEPS)[None, :] <= jnp.arange(STEPS)[:, None]

    def attend(pieces):
        group_keys, group_values, length_row, group_queries, group_fresh_keys, group_fresh_values = pieces
        owner_request = block_requests(length_row, OLD_BLOCKS)
        query_wide = group_queries.astype(jnp.float32).reshape(REQ_OLD, STEPS, KV, group_ratio, HD)
        cached = jnp.einsum('jmkrd,itkd->jkrmit', query_wide, group_keys.astype(jnp.float32)) * score_scale
        member = owner_request[None, :] == jnp.arange(REQ_OLD)[:, None]
        cached = jnp.where(member[:, None, None, None, :, None], cached, masked_low)
        fresh_part = jnp.einsum('jmkrd,jukd->jkrmu', query_wide, group_fresh_keys.astype(jnp.float32)) * score_scale
        fresh_part = jnp.where(causal, fresh_part, masked_low)
        peak_score = jnp.maximum(lax.optimization_barrier(jnp.max(cached, axis=(-2, -1))), lax.optimization_barrier(jnp.max(fresh_part, axis=-1)))
        cached_probs = jnp.exp(cached - peak_score[..., None, None])
        fresh_probs = jnp.exp(fresh_part - peak_score[..., None])
        denominator = lax.optimization_barrier(jnp.sum(cached_probs, axis=(-2, -1))) + lax.optimization_barrier(jnp.sum(fresh_probs, axis=-1))
        cached_weights = lax.optimization_barrier(cached_probs.astype(jnp.bfloat16)).astype(jnp.float32)
        fresh_weights = lax.optimization_barrier(fresh_probs.astype(jnp.bfloat16)).astype(jnp.float32)
        numerator = jnp.einsum('jkrmit,itkd->jkrmd', cached_weights, group_values.astype(jnp.float32))
        numerator = numerator + jnp.einsum('jkrmu,jukd->jkrmd', fresh_weights, group_fresh_values.astype(jnp.float32))
        result = numerator / denominator[..., None]
        return jnp.transpose(result, (0, 3, 1, 2, 4)).reshape(REQ_OLD, STEPS, QH * HD).astype(jnp.bfloat16)
    context = lax.map(attend, (key_blocks, value_blocks, lengths, queries.reshape(group_count, REQ_OLD, STEPS, QH, HD), fresh_keys.reshape(group_count, REQ_OLD, STEPS, KV, HD), fresh_values.reshape(group_count, REQ_OLD, STEPS, KV, HD)))
    context = context.reshape(REQUESTS, STEPS, QH * HD)
    return (context, migrate(old_keys, block_owner), migrate(old_values, block_owner))
```

```python
import functools
import jax
import jax.numpy as jnp
from jax import lax
from jax.experimental import pallas as pl
from jax.experimental.pallas import tpu as pltpu
from jax.sharding import PartitionSpec as P

HD = 128
QH = 64
KV = 8
theta_base = 1000000.0
eps_norm = 1e-06
masked_low = -1e30


def rotate(vectors, positions):
    half_dim = vectors.shape[-1] // 2
    frequency = theta_base ** (-2.0 * jnp.arange(half_dim, dtype=jnp.float32) / vectors.shape[-1])
    angles = positions[..., None, None] * frequency
    cosine = jnp.cos(angles)
    sine_part = jnp.sin(angles)
    lower_half = vectors[..., :half_dim]
    upper_half = vectors[..., half_dim:]
    return jnp.concatenate(
        [
            lower_half * cosine - upper_half * sine_part,
            upper_half * cosine + lower_half * sine_part,
        ],
        axis=-1,
    )


def attend_kernel(steps, heads, request_ref, q_ref, fk_ref, fv_ref, k_ref, v_ref, out_ref, held, fresh, top, total, accum):
    step = pl.program_id(0)
    blocks = held.shape[0]
    requests = q_ref.shape[0]
    rows = q_ref.shape[1] // heads
    ratio = rows // steps
    scale = HD ** (-0.5)
    contract = (((1,), (1,)), ((), ()))

    @pl.when(step == 0)
    def _():
        padded = fk_ref.shape[2]
        row_step = lax.broadcasted_iota(jnp.int32, (rows, padded), 0) // ratio
        column = lax.broadcasted_iota(jnp.int32, (rows, padded), 1)
        causal = (column <= row_step) & (column < steps)
        for j in range(requests):
            for h in range(heads):
                part = pl.ds(h * rows, rows)
                scores = lax.dot_general(
                    q_ref[j, part, :], fk_ref[j, h], contract, preferred_element_type=jnp.float32
                )
                scores = jnp.where(causal, scores * scale, masked_low)
                fresh[j, part, :] = scores
                peak = jnp.max(scores, axis=-1, keepdims=True)
                top[j, part, :] = jnp.broadcast_to(peak, (rows, HD))

    @pl.when(step < blocks)
    def _():
        j = request_ref[step]
        for h in range(heads):
            part = pl.ds(h * rows, rows)
            scores = (
                lax.dot_general(
                    q_ref[j, part, :],
                    k_ref[0, :, pl.ds(h * HD, HD)],
                    contract,
                    preferred_element_type=jnp.float32,
                )
                * scale
            )
            held[step, part, :] = scores
            top[j, part, :] = jnp.maximum(
                top[j, part, :], jnp.max(scores, axis=-1, keepdims=True)
            )

    @pl.when(step == blocks)
    def _():
        for j in range(requests):
            for h in range(heads):
                part = pl.ds(h * rows, rows)
                probs = jnp.exp(fresh[j, part, :] - top[j, part, :1])
                total[j, part, :] = jnp.broadcast_to(
                    jnp.sum(probs, axis=-1, keepdims=True), (rows, HD)
                )
                accum[j, part, :] = jnp.dot(
                    probs.astype(jnp.bfloat16), fv_ref[j, h], preferred_element_type=jnp.float32
                )

    @pl.when(step >= blocks)
    def _():
        j = request_ref[step - blocks]
        for h in range(heads):
            part = pl.ds(h * rows, rows)
            probs = jnp.exp(held[step - blocks, part, :] - top[j, part, :1])
            total[j, part, :] += jnp.sum(probs, axis=-1, keepdims=True)
            accum[j, part, :] += jnp.dot(
                probs.astype(jnp.bfloat16),
                v_ref[0, :, pl.ds(h * HD, HD)],
                preferred_element_type=jnp.float32,
            )

    @pl.when(step == pl.num_programs(0) - 1)
    def _():
        out_ref[...] = (accum[...] / total[...]).astype(out_ref.dtype)


def attend(request_of, queries, fresh_keys, fresh_values, keys, values, steps):
    requests, heads = fresh_keys.shape[:2]
    blocks, tokens, width = keys.shape
    whole = lambda shape: pl.BlockSpec(shape, lambda i, r: (0,) * len(shape))
    state = pltpu.VMEM(queries.shape, jnp.float32)
    return pl.pallas_call(
        functools.partial(attend_kernel, steps, heads),
        out_shape=jax.ShapeDtypeStruct(queries.shape, jnp.bfloat16),
        grid_spec=pltpu.PrefetchScalarGridSpec(
            num_scalar_prefetch=1,
            grid=(2 * blocks,),
            in_specs=[
                whole(queries.shape),
                whole(fresh_keys.shape),
                whole(fresh_values.shape),
                pl.BlockSpec(
                    (1, tokens, width), lambda i, r: (jnp.minimum(i, blocks - 1), 0, 0)
                ),
                pl.BlockSpec(
                    (1, tokens, width), lambda i, r: (jnp.maximum(i - blocks, 0), 0, 0)
                ),
            ],
            out_specs=whole(queries.shape),
            scratch_shapes=[
                pltpu.VMEM((blocks, queries.shape[1], tokens), jnp.float32),
                pltpu.VMEM(queries.shape[:2] + fresh_keys.shape[2:3], jnp.float32),
                state,
                state,
                state,
            ],
        ),
        compiler_params=pltpu.CompilerParams(vmem_limit_bytes=32 * 1024 * 1024),
        cost_estimate=pl.CostEstimate(
            flops=4 * queries.shape[1] * HD * tokens * blocks,
            bytes_accessed=4 * blocks * tokens * width,
            transcendentals=queries.shape[1] * tokens * blocks,
        ),
        name="attend",
    )(request_of, queries, fresh_keys, fresh_values, keys, values)


def settle(table, offset, count, arrivals, outs, buffers, sem):
    mine, other = arrivals
    width = mine[0].shape[-1]

    def inward(i, side):
        places = pl.ds(side * width, width), pl.ds((1 - side) * width, width)
        return [
            pltpu.make_async_copy(half[a].at[i], buffers[a].at[i, :, place], sem.at[i, 2 * a + s])
            for a in range(2)
            for s, (half, place) in enumerate(zip((mine, other), places))
        ]

    def outward(i):
        slot = table[offset + i]
        return [
            pltpu.make_async_copy(buffers[a].at[i], outs[a].at[slot], sem.at[i, 4 + a])
            for a in range(2)
        ]

    for side in range(2):

        @pl.when(table[core_at] == side)
        def _():
            for i in range(count):

                @pl.when(table[offset + i] >= 0)
                def _():
                    for copy in inward(i, side):
                        copy.start()

            for i in range(count):

                @pl.when(table[offset + i] >= 0)
                def _():
                    for copy in inward(i, side):
                        copy.wait()
                    for copy in outward(i):
                        copy.start()

            for i in range(count):

                @pl.when(table[offset + i] >= 0)
                def _():
                    for copy in outward(i):
                        copy.wait()


def place_kernel(offset, count, table, mine, other, kin_ref, vin_ref, k_out, v_out, kbuf, vbuf, sem):
    del kin_ref, vin_ref
    halves = [[ref.at[:, a] for a in range(2)] for ref in (mine, other)]
    settle(table, offset, count, halves, (k_out, v_out), (kbuf, vbuf), sem)


def place(table, offset, mine, other, pools):
    count = mine.shape[0]
    anywhere = pl.BlockSpec(memory_space=pl.ANY)
    buffer = pltpu.VMEM((count,) + pools[0].shape[1:], pools[0].dtype)
    return pl.pallas_call(
        functools.partial(place_kernel, offset, count),
        out_shape=[jax.ShapeDtypeStruct(a.shape, a.dtype) for a in pools],
        in_specs=[pl.BlockSpec(memory_space=pltpu.SMEM)] + [anywhere] * 4,
        out_specs=[anywhere] * 2,
        scratch_shapes=[buffer, buffer, pltpu.SemaphoreType.DMA((count, 6))],
        input_output_aliases={3: 0, 4: 1},
        compiler_params=pltpu.CompilerParams(vmem_limit_bytes=(4 + 2 * count) << 20),
        cost_estimate=pl.CostEstimate(
            flops=0, bytes_accessed=4 * mine.size, transcendentals=0
        ),
        name="place",
    )(table, mine, other, *pools)


def home_kernel(table, km_ref, vm_ref, ko_ref, vo_ref, k_out, v_out, kbuf, vbuf, blank, sem, blank_sem):
    slots = k_out.shape[0]
    blank[...] = jnp.zeros_like(blank)

    def clearing(i):
        return [
            pltpu.make_async_copy(blank, out.at[i], blank_sem.at[i, a])
            for a, out in enumerate((k_out, v_out))
        ]

    for i in range(slots):

        @pl.when(i >= table[filled_at])
        def _():
            for copy in clearing(i):
                copy.start()

    halves = ((km_ref, vm_ref), (ko_ref, vo_ref))
    settle(table, home_at, km_ref.shape[0], halves, (k_out, v_out), (kbuf, vbuf), sem)
    for i in range(slots):

        @pl.when(i >= table[filled_at])
        def _():
            for copy in clearing(i):
                copy.wait()


def place_home(table, mine, other, slot_count):
    blocks, block_tokens, width = mine[0].shape
    anywhere = pl.BlockSpec(memory_space=pl.ANY)
    buffer = pltpu.VMEM((blocks, block_tokens, 2 * width), mine[0].dtype)
    pool = jax.ShapeDtypeStruct((slot_count, block_tokens, 2 * width), mine[0].dtype)
    return pl.pallas_call(
        home_kernel,
        out_shape=[pool, pool],
        in_specs=[pl.BlockSpec(memory_space=pltpu.SMEM)] + [anywhere] * 4,
        out_specs=[anywhere] * 2,
        scratch_shapes=[
            buffer,
            buffer,
            pltpu.VMEM((block_tokens, 2 * width), mine[0].dtype),
            pltpu.SemaphoreType.DMA((blocks, 6)),
            pltpu.SemaphoreType.DMA((slot_count, 2)),
        ],
        compiler_params=pltpu.CompilerParams(vmem_limit_bytes=(6 + 2 * blocks) << 20),
        cost_estimate=pl.CostEstimate(
            flops=0, bytes_accessed=4 * mine[0].size * 2, transcendentals=0
        ),
        name="place_home",
    )(table, *mine, *other)


own_at, home_at, far_at, core_at, filled_at = 0, 16, 32, 48, 49


def plan_kernel(owner_ref, rank_ref, table):
    rank = rank_ref[0]
    parity = rank // 2
    for i in range(table.shape[0]):
        table[i] = 0
    for i in range(far_at, core_at):
        table[i] = -1
    slot, leaving, coming = 0, 0, 0
    for p in range(2):
        own = (parity == p).astype(jnp.int32)
        for i in range(owner_ref.shape[1]):
            owner = owner_ref[p, i]
            mine = owner == rank
            value = jnp.where(mine, slot, -1)
            slot = slot + mine.astype(jnp.int32)
            crossing = (owner // 2 != p).astype(jnp.int32)

            @pl.when(own == 1)
            def _():
                table[home_at + i] = value

            @pl.when(own * crossing == 1)
            def _():
                table[own_at + leaving] = i

            @pl.when((1 - own) * crossing == 1)
            def _():
                table[far_at + coming] = value

            leaving = leaving + own * crossing
            coming = coming + (1 - own) * crossing
    table[core_at] = rank % 2
    table[filled_at] = slot


def plan(block_owner, rank):
    scalars = pl.BlockSpec(memory_space=pltpu.SMEM)
    return pl.pallas_call(
        plan_kernel,
        out_shape=jax.ShapeDtypeStruct((64,), jnp.int32),
        in_specs=[scalars, scalars],
        out_specs=scalars,
        name="plan",
    )(block_owner, rank[None].astype(jnp.int32))


def gather_kernel(table, k_ref, v_ref, *outs):
    for at, out in enumerate(outs):

        @pl.when(pl.program_id(0) == at)
        def _():
            out[0, 0] = k_ref[0]
            out[0, 1] = v_ref[0]


def gather(table, offset, sizes, sources):
    count = sum(sizes)
    shape = (1,) + sources[0].shape[1:]
    taken = pl.BlockSpec(shape, lambda i, table: (table[offset + i], 0, 0))
    starts = [sum(sizes[:i]) for i in range(len(sizes))]
    return pl.pallas_call(
        gather_kernel if len(sizes) > 1 else gather_one_kernel,
        out_shape=[
            jax.ShapeDtypeStruct((size, 2) + shape[1:], sources[0].dtype) for size in sizes
        ],
        grid_spec=pltpu.PrefetchScalarGridSpec(
            num_scalar_prefetch=1,
            grid=(count,),
            in_specs=[taken, taken],
            out_specs=[
                pl.BlockSpec(
                    (1, 2) + shape[1:],
                    lambda i, table, size=size, start=start: (
                        jnp.clip(i - start, 0, size - 1),
                        0,
                        0,
                        0,
                    ),
                )
                for size, start in zip(sizes, starts)
            ],
        ),
        cost_estimate=pl.CostEstimate(
            flops=0, bytes_accessed=8 * count * sources[0][0].size, transcendentals=0
        ),
        compiler_params=pltpu.CompilerParams(vmem_limit_bytes=40 << 20),
        name="gather",
    )(table, *sources)


def gather_one_kernel(table, k_ref, v_ref, out):
    out[0, 0] = k_ref[0]
    out[0, 1] = v_ref[0]


def project(tokens, q_weight, kv_weight, block_tokens, lengths, rank, n):
    parity = rank // (n // 2)
    row_count, steps, depth = tokens.shape
    widened = tokens.astype(jnp.float32)
    normed = (
        widened * lax.rsqrt(jnp.mean(widened * widened, axis=-1, keepdims=True) + eps_norm)
    ).astype(jnp.bfloat16)
    flattened = normed.reshape(row_count * steps, depth)
    query_part = jnp.dot(flattened, q_weight, preferred_element_type=jnp.float32).astype(jnp.bfloat16)
    pair_part = jnp.dot(flattened, kv_weight, preferred_element_type=jnp.float32).astype(jnp.bfloat16)
    query_part, pair_part = lax.optimization_barrier((query_part, pair_part))
    starts = (lengths.reshape(-1) * block_tokens).astype(jnp.float32)
    positions = starts[:, None] + jnp.arange(steps, dtype=jnp.float32)[None, :]

    def turned(rows):
        shaped = rows.astype(jnp.float32).reshape(row_count, steps, -1, HD)
        return rotate(shaped, positions).astype(jnp.bfloat16).reshape(rows.shape)

    queries = turned(query_part)
    pairs = jnp.where(parity == 0, turned(pair_part), pair_part)
    return queries, pairs


def head_routes(n):
    w = n // 2
    return [[(t, ((t + flip) % 2) * w + t // 2) for t in range(n)] for flip in range(2)]


def exchange(queries, pairs, lengths, rank, n):
    w = n // 2
    parity, core = rank // w, rank % 2
    per_group = lengths.shape[1]
    steps = queries.shape[0] // (2 * per_group)
    heads = KV // w
    ratio = QH // KV
    group_rows = per_group * steps

    def group_of(rows, which):
        return lax.dynamic_slice_in_dim(rows, which * group_rows, group_rows, 0)

    to_same, to_cross = head_routes(n)
    same = lax.ppermute(group_of(queries, core), "tensor", to_same)
    cross = lax.ppermute(group_of(queries, 1 - core), "tensor", to_cross)
    own_pair = group_of(pairs, parity)
    far_pair = lax.ppermute(
        group_of(pairs, 1 - parity), "tensor", [(t, (t + w) % n) for t in range(n)]
    )
    first = jnp.where(parity == 0, same, cross)
    second = jnp.where(parity == 0, cross, same)
    held = jnp.concatenate([first, second], axis=1).reshape(per_group, steps, heads, ratio, HD)
    held = jnp.transpose(held, (0, 2, 1, 3, 4)).reshape(per_group, heads * steps * ratio, HD)

    def fresh(rows):
        shaped = jnp.transpose(rows.reshape(per_group, steps, heads, HD), (0, 2, 1, 3))
        return jnp.pad(shaped, ((0, 0), (0, 0), (0, 16 - steps), (0, 0)))

    fresh_keys = fresh(jnp.where(parity == 0, own_pair, far_pair))
    fresh_values = fresh(jnp.where(parity == 0, far_pair, own_pair))
    return held, fresh_keys, fresh_values


def attention(held, fresh_keys, fresh_values, keys, values, lengths, steps, rank, n):
    parity, core = rank // (n // 2), rank % 2
    per_group, heads = fresh_keys.shape[:2]
    blocks = keys.shape[0]
    ratio = QH // KV
    group_rows = per_group * steps
    to_same, to_cross = head_routes(n)
    own_lengths = jnp.where(parity == 0, lengths[0], lengths[1])
    ends = jnp.cumsum(own_lengths)
    request_of = jnp.sum(
        (jnp.arange(blocks)[:, None] >= ends[None, :]).astype(jnp.int32), axis=1
    )
    out = attend(request_of, held, fresh_keys, fresh_values, keys, values, steps)
    out = jnp.transpose(out.reshape(per_group, heads, steps, ratio * HD), (0, 2, 1, 3))
    out = out.reshape(group_rows, heads * ratio * HD)
    width = heads * ratio * HD // 2
    lower, upper = out[:, :width], out[:, width:]
    back_same = lax.ppermute(
        jnp.where(parity == 0, lower, upper), "tensor", [(d, t) for t, d in to_same]
    )
    back_cross = lax.ppermute(
        jnp.where(parity == 0, upper, lower), "tensor", [(d, t) for t, d in to_cross]
    )
    groups = [jnp.where(core == 0, back_same, back_cross), jnp.where(core == 0, back_cross, back_same)]
    return jnp.concatenate(groups, axis=0).reshape(2 * per_group, steps, width)


head_sizes = (2, 2)
tie = lax.optimization_barrier


def finish_two_chips(total, operands):
    table, keys, values, home, head, ready = operands
    n = lax.axis_size("tensor")
    slot_count = 8 * keys.shape[0] // (3 * n)
    chip_pairs = [(t, (t + 2) % n) for t in range(n)]
    core_pairs = [(t, t ^ 1) for t in range(n)]
    low = sum(head_sizes)
    parts = [(0, *head[0]), (head_sizes[0], head[1], None)]
    arrived = []
    for i in range(total - low):
        sent = ready[i]
        if i >= 3:
            sent, arrived[i - 3] = tie((sent, arrived[i - 3]))
        arrived.append(lax.ppermute(sent, "tensor", chip_pairs))
    if arrived:
        home, arrived[0] = tie((home, arrived[0]))
    parts += [(low + i, mine, None) for i, mine in enumerate(arrived)]
    pools = place_home(table, (keys, values), home, slot_count)
    waiting = None
    for at, mine, other in parts:
        if other is None:
            mine, pools = tie((mine, pools))
            other = lax.ppermute(mine, "tensor", core_pairs)
        if waiting is not None:
            pools = place(table, *waiting, pools)
        waiting = (far_at + at, mine, other)
    return place(table, *waiting, pools)


def two_chips(tokens, q_weight, kv_weight, keys, values, lengths, block_owner, rank, n):
    chip_pairs = [(t, (t + 2) % n) for t in range(n)]
    core_pairs = [(t, t ^ 1) for t in range(n)]
    table = plan(block_owner, rank)
    (first,) = gather(table, own_at, head_sizes[:1], (keys, values))
    block_owner, first = tie((block_owner, first))
    coming = lax.ppermute(first, "tensor", chip_pairs)
    home = [lax.ppermute(a, "tensor", core_pairs) for a in (keys, values)]
    everyone = lax.all_gather(block_owner, ("groups", "batch"))
    crossing = jnp.sum(
        (everyone // 2 != jnp.arange(2)[None, :, None]).astype(jnp.int32), axis=2
    )
    most = jnp.max(crossing)
    tokens, most = tie((tokens, most))
    queries, pairs = project(tokens, q_weight, kv_weight, keys.shape[1], lengths, rank, n)
    (second,) = gather(table, own_at + head_sizes[0], head_sizes[1:], (keys, values))
    queries, pairs, second, *home = tie((queries, pairs, second, *home))
    held = exchange(queries, pairs, lengths, rank, n)
    second, *held = tie((second, *held))
    later = lax.ppermute(second, "tensor", chip_pairs)
    context = attention(*held, keys, values, lengths, tokens.shape[1], rank, n)
    low = sum(head_sizes)
    ready = gather(table, own_at + low, (1,) * (keys.shape[0] - low), (keys, values))
    coming, held = tie((coming, held))
    head = [(coming, lax.ppermute(coming, "tensor", core_pairs)), later]
    totals = [5, 7, 8, 9, 10, 11, 12]
    which = jnp.sum((most > jnp.array(totals[:-1])).astype(jnp.int32))
    which, context = tie((which, context))
    operands = (table, keys, values, home, head, ready)
    new_keys, new_values = lax.switch(
        which, [functools.partial(finish_two_chips, total) for total in totals], operands
    )
    return context, new_keys, new_values


def move_padded(keys, values, block_owner, rank, n):
    parity = rank // (n // 2)
    blocks, block_tokens, width = keys.shape
    slot_count = 8 * blocks // (3 * n)
    own_owner = jnp.where(parity == 0, block_owner[0], block_owner[1])
    block_ids = jnp.arange(blocks)
    slot_ids = jnp.arange(slot_count)
    same_owner = own_owner[:, None] == own_owner[None, :]
    block_rank = jnp.sum(
        (same_owner & (block_ids[:, None] > block_ids[None, :])).astype(jnp.int32), axis=1
    )
    chosen = (own_owner[None, None, :] == jnp.arange(n)[None, :, None]) & (
        block_rank[None, None, :] == slot_ids[:, None, None]
    )
    selector = chosen.astype(jnp.bfloat16)
    counts = jnp.sum((block_owner == rank).astype(jnp.int32), axis=1)
    target = jnp.stack([slot_ids, counts[0] + slot_ids])
    filled = slot_ids[None, :] < counts[:, None]
    placement = ((target[None] == slot_ids[:, None, None]) & filled[None]).astype(jnp.bfloat16)
    moved = []
    for pool in (keys, values):
        send = jnp.einsum(
            "cdi,itl->cdtl", selector, pool, preferred_element_type=jnp.float32
        ).astype(jnp.bfloat16)
        got = lax.all_to_all(send, "tensor", split_axis=1, concat_axis=3, tiled=True)
        unpacked = got.reshape(slot_count, block_tokens, 2, KV * HD)
        moved.append(
            jnp.einsum(
                "spc,ctpl->stl", placement, unpacked, preferred_element_type=jnp.float32
            ).astype(jnp.bfloat16)
        )
    return moved


def per_device(tokens, q_weight, kv_weight, old_keys, old_values, lengths, block_owner):
    n = lax.axis_size("tensor")
    rank = lax.axis_index("tensor")
    keys, values = old_keys[0], old_values[0]
    if n == 4:
        context, new_keys, new_values = two_chips(
            tokens, q_weight, kv_weight, keys, values, lengths, block_owner, rank, n
        )
    else:
        new_keys, new_values = move_padded(keys, values, block_owner, rank, n)
        queries, pairs = project(tokens, q_weight, kv_weight, keys.shape[1], lengths, rank, n)
        held = exchange(queries, pairs, lengths, rank, n)
        context = attention(*held, keys, values, lengths, tokens.shape[1], rank, n)
    return (context, new_keys[None], new_values[None])


def solution(mesh):
    return jax.shard_map(
        per_device,
        mesh=mesh,
        in_specs=(
            P(("groups", "batch"), None, None),
            P(None, "tensor"),
            P(None, "tensor"),
            P("tensor", ("groups", "batch"), None, None),
            P("tensor", ("groups", "batch"), None, None),
            P(("groups", "batch"), None),
            P(("groups", "batch"), None),
        ),
        out_specs=(
            P(("groups", "batch"), None, "tensor"),
            P(("groups", "batch"), "tensor", None, None),
            P(("groups", "batch"), "tensor", None, None),
        ),
        check_vma=False,
    )
```

```python
import functools
import jax
import jax.numpy as jnp
from jax import lax
from jax.experimental import pallas as pl
from jax.experimental.pallas import tpu as pltpu
from jax.sharding import PartitionSpec as P

HD = 128
QH = 64
KV = 8
theta_base = 1000000.0
eps_norm = 1e-06
masked_low = -1e30


def rotate(vectors, positions):
    half_dim = vectors.shape[-1] // 2
    frequency = theta_base ** (-2.0 * jnp.arange(half_dim, dtype=jnp.float32) / vectors.shape[-1])
    angles = positions[..., None, None] * frequency
    cosine = jnp.cos(angles)
    sine_part = jnp.sin(angles)
    lower_half = vectors[..., :half_dim]
    upper_half = vectors[..., half_dim:]
    return jnp.concatenate(
        [
            lower_half * cosine - upper_half * sine_part,
            upper_half * cosine + lower_half * sine_part,
        ],
        axis=-1,
    )


def attend_kernel(steps, heads, request_ref, q_ref, fk_ref, fv_ref, k_ref, v_ref, out_ref, held, fresh, top, total, accum):
    step = pl.program_id(0)
    blocks = held.shape[0]
    requests = q_ref.shape[0]
    rows = q_ref.shape[1] // heads
    ratio = rows // steps
    scale = HD ** (-0.5)
    contract = (((1,), (1,)), ((), ()))

    @pl.when(step == 0)
    def _():
        padded = fk_ref.shape[2]
        row_step = lax.broadcasted_iota(jnp.int32, (rows, padded), 0) // ratio
        column = lax.broadcasted_iota(jnp.int32, (rows, padded), 1)
        causal = (column <= row_step) & (column < steps)
        for j in range(requests):
            for h in range(heads):
                part = pl.ds(h * rows, rows)
                scores = lax.dot_general(
                    q_ref[j, part, :], fk_ref[j, h], contract, preferred_element_type=jnp.float32
                )
                scores = jnp.where(causal, scores * scale, masked_low)
                fresh[j, part, :] = scores
                peak = jnp.max(scores, axis=-1, keepdims=True)
                top[j, part, :] = jnp.broadcast_to(peak, (rows, HD))

    @pl.when(step < blocks)
    def _():
        j = request_ref[step]
        for h in range(heads):
            part = pl.ds(h * rows, rows)
            scores = (
                lax.dot_general(
                    q_ref[j, part, :],
                    k_ref[0, :, pl.ds(h * HD, HD)],
                    contract,
                    preferred_element_type=jnp.float32,
                )
                * scale
            )
            held[step, part, :] = scores
            top[j, part, :] = jnp.maximum(
                top[j, part, :], jnp.max(scores, axis=-1, keepdims=True)
            )

    @pl.when(step == blocks)
    def _():
        for j in range(requests):
            for h in range(heads):
                part = pl.ds(h * rows, rows)
                probs = jnp.exp(fresh[j, part, :] - top[j, part, :1])
                total[j, part, :] = jnp.broadcast_to(
                    jnp.sum(probs, axis=-1, keepdims=True), (rows, HD)
                )
                accum[j, part, :] = jnp.dot(
                    probs.astype(jnp.bfloat16), fv_ref[j, h], preferred_element_type=jnp.float32
                )

    @pl.when(step >= blocks)
    def _():
        j = request_ref[step - blocks]
        for h in range(heads):
            part = pl.ds(h * rows, rows)
            probs = jnp.exp(held[step - blocks, part, :] - top[j, part, :1])
            total[j, part, :] += jnp.sum(probs, axis=-1, keepdims=True)
            accum[j, part, :] += jnp.dot(
                probs.astype(jnp.bfloat16),
                v_ref[0, :, pl.ds(h * HD, HD)],
                preferred_element_type=jnp.float32,
            )

    @pl.when(step == pl.num_programs(0) - 1)
    def _():
        out_ref[...] = (accum[...] / total[...]).astype(out_ref.dtype)


def attend(request_of, queries, fresh_keys, fresh_values, keys, values, steps):
    requests, heads = fresh_keys.shape[:2]
    blocks, tokens, width = keys.shape
    whole = lambda shape: pl.BlockSpec(shape, lambda i, r: (0,) * len(shape))
    state = pltpu.VMEM(queries.shape, jnp.float32)
    return pl.pallas_call(
        functools.partial(attend_kernel, steps, heads),
        out_shape=jax.ShapeDtypeStruct(queries.shape, jnp.bfloat16),
        grid_spec=pltpu.PrefetchScalarGridSpec(
            num_scalar_prefetch=1,
            grid=(2 * blocks,),
            in_specs=[
                whole(queries.shape),
                whole(fresh_keys.shape),
                whole(fresh_values.shape),
                pl.BlockSpec(
                    (1, tokens, width), lambda i, r: (jnp.minimum(i, blocks - 1), 0, 0)
                ),
                pl.BlockSpec(
                    (1, tokens, width), lambda i, r: (jnp.maximum(i - blocks, 0), 0, 0)
                ),
            ],
            out_specs=whole(queries.shape),
            scratch_shapes=[
                pltpu.VMEM((blocks, queries.shape[1], tokens), jnp.float32),
                pltpu.VMEM(queries.shape[:2] + fresh_keys.shape[2:3], jnp.float32),
                state,
                state,
                state,
            ],
        ),
        compiler_params=pltpu.CompilerParams(vmem_limit_bytes=32 * 1024 * 1024),
        cost_estimate=pl.CostEstimate(flops=0, bytes_accessed=4096, transcendentals=0),
        name="attend",
    )(request_of, queries, fresh_keys, fresh_values, keys, values)


def settle(table, offset, count, arrivals, outs, buffers, sem):
    mine, other = arrivals
    width = mine[0].shape[-1]

    def inward(i, side):
        places = pl.ds(side * width, width), pl.ds((1 - side) * width, width)
        return [
            pltpu.make_async_copy(half[a].at[i], buffers[a].at[i, :, place], sem.at[i, 2 * a + s])
            for a in range(2)
            for s, (half, place) in enumerate(zip((mine, other), places))
        ]

    def outward(i):
        slot = table[offset + i]
        return [
            pltpu.make_async_copy(buffers[a].at[i], outs[a].at[slot], sem.at[i, 4 + a])
            for a in range(2)
        ]

    for side in range(2):

        @pl.when(table[core_at] == side)
        def _():
            for i in range(count):

                @pl.when(table[offset + i] >= 0)
                def _():
                    for copy in inward(i, side):
                        copy.start()

            for i in range(count):

                @pl.when(table[offset + i] >= 0)
                def _():
                    for copy in inward(i, side):
                        copy.wait()
                    for copy in outward(i):
                        copy.start()

            for i in range(count):

                @pl.when(table[offset + i] >= 0)
                def _():
                    for copy in outward(i):
                        copy.wait()


def place_kernel(offset, count, table, mine, other, kin_ref, vin_ref, k_out, v_out, kbuf, vbuf, sem):
    del kin_ref, vin_ref
    halves = [[ref.at[:, a] for a in range(2)] for ref in (mine, other)]
    settle(table, offset, count, halves, (k_out, v_out), (kbuf, vbuf), sem)


def place(table, offset, mine, other, pools):
    count = mine.shape[0]
    anywhere = pl.BlockSpec(memory_space=pl.ANY)
    buffer = pltpu.VMEM((count,) + pools[0].shape[1:], pools[0].dtype)
    return pl.pallas_call(
        functools.partial(place_kernel, offset, count),
        out_shape=[jax.ShapeDtypeStruct(a.shape, a.dtype) for a in pools],
        in_specs=[pl.BlockSpec(memory_space=pltpu.SMEM)] + [anywhere] * 4,
        out_specs=[anywhere] * 2,
        scratch_shapes=[buffer, buffer, pltpu.SemaphoreType.DMA((count, 6))],
        input_output_aliases={3: 0, 4: 1},
        compiler_params=pltpu.CompilerParams(vmem_limit_bytes=(4 + 2 * count) << 20),
        cost_estimate=pl.CostEstimate(flops=0, bytes_accessed=4096, transcendentals=0),
        name="place",
    )(table, mine, other, *pools)


def home_kernel(table, km_ref, vm_ref, ko_ref, vo_ref, k_out, v_out, kbuf, vbuf, blank, sem, blank_sem):
    slots = k_out.shape[0]
    blank[...] = jnp.zeros_like(blank)

    def clearing(i):
        return [
            pltpu.make_async_copy(blank, out.at[i], blank_sem.at[i, a])
            for a, out in enumerate((k_out, v_out))
        ]

    for i in range(slots):

        @pl.when(i >= table[filled_at])
        def _():
            for copy in clearing(i):
                copy.start()

    halves = ((km_ref, vm_ref), (ko_ref, vo_ref))
    settle(table, home_at, km_ref.shape[0], halves, (k_out, v_out), (kbuf, vbuf), sem)
    for i in range(slots):

        @pl.when(i >= table[filled_at])
        def _():
            for copy in clearing(i):
                copy.wait()


def place_home(table, mine, other, slot_count):
    blocks, block_tokens, width = mine[0].shape
    anywhere = pl.BlockSpec(memory_space=pl.ANY)
    buffer = pltpu.VMEM((blocks, block_tokens, 2 * width), mine[0].dtype)
    pool = jax.ShapeDtypeStruct((slot_count, block_tokens, 2 * width), mine[0].dtype)
    return pl.pallas_call(
        home_kernel,
        out_shape=[pool, pool],
        in_specs=[pl.BlockSpec(memory_space=pltpu.SMEM)] + [anywhere] * 4,
        out_specs=[anywhere] * 2,
        scratch_shapes=[
            buffer,
            buffer,
            pltpu.VMEM((block_tokens, 2 * width), mine[0].dtype),
            pltpu.SemaphoreType.DMA((blocks, 6)),
            pltpu.SemaphoreType.DMA((slot_count, 2)),
        ],
        compiler_params=pltpu.CompilerParams(vmem_limit_bytes=(6 + 2 * blocks) << 20),
        cost_estimate=pl.CostEstimate(flops=0, bytes_accessed=4096, transcendentals=0),
        name="place_home",
    )(table, *mine, *other)


own_at, home_at, far_at, core_at, filled_at, lent_at = 0, 16, 32, 48, 49, 52
pick_at, place_at, give_at, back_at, table_size = 64, 80, 96, 104, 128
lent = 2
ahead = 3


def plan_kernel(owner_ref, rank_ref, table):
    rank = rank_ref[0]
    parity = rank // 2
    for i in range(table.shape[0]):
        table[i] = 0
    for i in range(far_at, core_at):
        table[i] = -1
    slot, leaving, coming = jnp.int32(0), jnp.int32(0), jnp.int32(0)
    for p in range(2):
        own = (parity == p).astype(jnp.int32)
        for i in range(owner_ref.shape[1]):
            owner = owner_ref[p, i]
            mine = owner == rank
            value = jnp.where(mine, slot, -1)
            slot = slot + mine.astype(jnp.int32)
            crossing = (owner // 2 != p).astype(jnp.int32)

            @pl.when(own == 1)
            def _():
                table[home_at + i] = value

            @pl.when(own * crossing == 1)
            def _():
                table[own_at + leaving] = i

            @pl.when((1 - own) * crossing == 1)
            def _():
                table[far_at + coming] = value

            leaving = leaving + own * crossing
            coming = coming + (1 - own) * crossing
    table[core_at] = rank % 2
    table[filled_at] = slot
    for i in range(lent_at, pick_at):
        table[i] = table[own_at + jnp.maximum(leaving - 1 - (i - lent_at), 0)]


def plan(block_owner, rank):
    scalars = pl.BlockSpec(memory_space=pltpu.SMEM)
    return pl.pallas_call(
        plan_kernel,
        out_shape=jax.ShapeDtypeStruct((64,), jnp.int32),
        in_specs=[scalars, scalars],
        out_specs=scalars,
        name="plan",
    )(block_owner, rank[None].astype(jnp.int32))


def gather_kernel(starts, table, k_ref, v_ref, *outs):
    for start, end, out in zip(starts[:-1], starts[1:], outs):

        @pl.when((pl.program_id(0) >= start) & (pl.program_id(0) < end))
        def _():
            out[0, 0] = k_ref[0]
            out[0, 1] = v_ref[0]


def gather(table, offset, sizes, sources):
    count = sum(sizes)
    shape = (1,) + sources[0].shape[1:]
    taken = pl.BlockSpec(shape, lambda i, table: (table[offset + i], 0, 0))
    starts = [sum(sizes[:i]) for i in range(len(sizes) + 1)]
    return pl.pallas_call(
        functools.partial(gather_kernel, starts),
        out_shape=[
            jax.ShapeDtypeStruct((size, 2) + shape[1:], sources[0].dtype) for size in sizes
        ],
        grid_spec=pltpu.PrefetchScalarGridSpec(
            num_scalar_prefetch=1,
            grid=(count,),
            in_specs=[taken, taken],
            out_specs=[
                pl.BlockSpec(
                    (1, 2) + shape[1:],
                    lambda i, table, size=size, start=start: (
                        jnp.clip(i - start, 0, size - 1),
                        0,
                        0,
                        0,
                    ),
                )
                for size, start in zip(sizes, starts)
            ],
        ),
        cost_estimate=pl.CostEstimate(flops=0, bytes_accessed=4096, transcendentals=0),
        compiler_params=pltpu.CompilerParams(vmem_limit_bytes=40 << 20),
        name="gather",
    )(table, *sources)


def route_kernel(edges, count_ref, flow_out, total_out):
    rows = count_ref.shape[0]
    lane = lax.broadcasted_iota(jnp.int32, (1, 128), 1)
    total, direction = lane & 15, lane >> 4
    counts = [jnp.where(direction == 0, count_ref[r, 0], count_ref[r, 1]) for r in range(rows)]
    excess = [jnp.maximum(c - total, 0) for c in counts]
    free = [jnp.maximum(total - jnp.maximum(c, ahead + 1), 0) for c in counts]
    width = len(edges)
    flow = [[jnp.zeros((1, 128), jnp.int32) for _ in range(width)] for _ in range(rows)]
    limit = [
        [jnp.clip(c - ahead - lent * k, 0, lent) for k in range(width)] for c in counts
    ]
    for _ in range(lent * width):
        for r in range(rows):
            marks = []
            for k, edge in enumerate(edges):
                near = edge[r]
                if near < 0:
                    marks.append(jnp.zeros((1, 128), jnp.int32))
                    continue
                can = (flow[r][k] < limit[r][k]) & (free[near] > 0) & (excess[r] > 0)
                marks.append(jnp.where(can, free[near] * 4 + 3 - k, 0))
            best = functools.reduce(jnp.maximum, marks)
            for k, edge in enumerate(edges):
                near = edge[r]
                if near >= 0:
                    took = jnp.where((marks[k] == best) & (best > 0), 1, 0)
                    flow[r][k] = flow[r][k] + took
                    free[near] = free[near] - took
                    excess[r] = excess[r] - took
    left = functools.reduce(jnp.maximum, excess)
    wrong = (left > 0) & (direction < 2) & (total <= 12)
    total_out[0] = jnp.max(jnp.where(wrong, total, 0)) + 1
    flow_out[...] = jnp.zeros_like(flow_out)
    for r in range(rows):
        for k in range(width):
            flow_out[pl.ds(r * width + k, 1), :] = flow[r][k]


def route(edges, counts):
    rows = counts.shape[0]
    height = -(-rows * len(edges) // 8) * 8
    return pl.pallas_call(
        functools.partial(route_kernel, edges),
        out_shape=[
            jax.ShapeDtypeStruct((height, 128), jnp.int32),
            jax.ShapeDtypeStruct((1,), jnp.int32),
        ],
        in_specs=[pl.BlockSpec(memory_space=pltpu.SMEM)],
        out_specs=[
            pl.BlockSpec(memory_space=pltpu.VMEM),
            pl.BlockSpec(memory_space=pltpu.SMEM),
        ],
        name="route",
    )(counts)


def assign_kernel(width, least, flow_ref, total_ref, count_ref, base_ref, place_ref, table):
    row, rank = place_ref[0], place_ref[1]
    parity = rank // 2
    total = jnp.maximum(total_ref[0], least)
    for i in range(pick_at):
        table[i] = base_ref[i]
    for i in range(pick_at, place_at):
        table[i] = 0
    for i in range(place_at, table_size):
        table[i] = -1
    for side in range(2):
        direction = parity if side == 0 else 1 - parity
        lane = total + 16 * direction
        count = count_ref[row, direction]
        slot = jnp.int32(0)
        for j in range(lent):
            for k in range(width):
                near = place_ref[2 + k]
                helped = (near >= 0) & (flow_ref[jnp.maximum(near, 0) * width + k, lane] > j)

                @pl.when(helped)
                def _():
                    if side == 0:
                        table[pick_at + slot] = 64 * (k + 1) + j
                    else:
                        table[give_at + j * width + k] = slot

                slot = slot + helped.astype(jnp.int32)
        blocks = home_at - 4
        for position in range(blocks):
            after = jnp.maximum(count - 1 - position, 0)
            k, j = after // lent, after % lent
            handed = (k < width) & (flow_ref[row * width + jnp.minimum(k, width - 1), lane] > j)
            held = position < count
            direct = held & jnp.logical_not(handed) & (position >= ahead)

            @pl.when(direct)
            def _():
                if side == 0:
                    table[pick_at + slot] = base_ref[own_at + position]
                else:
                    table[place_at + ahead + slot] = base_ref[far_at + position]

            if side == 1:

                @pl.when(held & handed)
                def _():
                    table[back_at + j * width + k] = base_ref[far_at + position]

                if position < ahead:

                    @pl.when(held)
                    def _():
                        table[place_at + position] = base_ref[far_at + position]

            slot = slot + direct.astype(jnp.int32)


def assign(width, least, flow, total, counts, base, places):
    scalars = pl.BlockSpec(memory_space=pltpu.SMEM)
    return pl.pallas_call(
        functools.partial(assign_kernel, width, least),
        out_shape=jax.ShapeDtypeStruct((table_size,), jnp.int32),
        in_specs=[scalars] * 5,
        out_specs=scalars,
        name="assign",
    )(flow, total, counts, base, places)


def pick_kernel(offset, sizes, sources, table, k_ref, v_ref, *rest):
    lent_refs, outs = rest[:sources], rest[sources : sources + len(sizes)]
    buffer, sem, out_sem = rest[sources + len(sizes) :]
    spots = [(out, at) for out, size in zip(outs, sizes) for at in range(size)]

    def inward(i, kind):
        index = table[pick_at + offset + i] & 63
        if kind == 0:
            pair = k_ref.at[index], v_ref.at[index]
        else:
            pair = lent_refs[kind - 1].at[index, 0], lent_refs[kind - 1].at[index, 1]
        return [pltpu.make_async_copy(pair[a], buffer.at[i, a], sem.at[i, a]) for a in range(2)]

    def outward(i):
        out, at = spots[i]
        return pltpu.make_async_copy(buffer.at[i], out.at[at], out_sem.at[i])

    for phase in range(2):
        for i in range(len(spots)):
            for kind in range(sources + 1):

                @pl.when(table[pick_at + offset + i] >> 6 == kind)
                def _():
                    for copy in inward(i, kind):
                        if phase == 0:
                            copy.start()
                        else:
                            copy.wait()

            if phase == 1:
                outward(i).start()
    for i in range(len(spots)):
        outward(i).wait()


def pick(table, offset, sizes, own, borrowed):
    scalars = pl.BlockSpec(memory_space=pltpu.SMEM)
    anywhere = pl.BlockSpec(memory_space=pl.ANY)
    count = sum(sizes)
    shape = (2,) + own[0].shape[1:]
    return pl.pallas_call(
        functools.partial(pick_kernel, offset, sizes, len(borrowed)),
        out_shape=[jax.ShapeDtypeStruct((size,) + shape, own[0].dtype) for size in sizes],
        in_specs=[scalars] + [anywhere] * (2 + len(borrowed)),
        out_specs=[anywhere] * len(sizes),
        scratch_shapes=[
            pltpu.VMEM((count,) + shape, own[0].dtype),
            pltpu.SemaphoreType.DMA((count, 2)),
            pltpu.SemaphoreType.DMA((count,)),
        ],
        compiler_params=pltpu.CompilerParams(vmem_limit_bytes=(4 + count) << 20),
        cost_estimate=pl.CostEstimate(flops=0, bytes_accessed=4096, transcendentals=0),
        name="pick",
    )(table, *own, *borrowed)


def give_kernel(offset, width, spots, table, *rest):
    many = 1 + max(array for array, _ in spots)
    arrivals, outs = rest[:many], rest[many : many + width]
    buffer, sem, out_sem = rest[many + width :]

    def inward(k, choice):
        array, at = spots[choice]
        return pltpu.make_async_copy(arrivals[array].at[at], buffer.at[k], sem.at[k])

    def outward(k):
        return pltpu.make_async_copy(buffer.at[k], outs[k].at[0], out_sem.at[k])

    for phase in range(3):
        for k in range(width):
            for choice in range(len(spots)):

                @pl.when(table[offset + k] == choice)
                def _():
                    if phase == 0:
                        inward(k, choice).start()
                    elif phase == 1:
                        inward(k, choice).wait()
                        outward(k).start()
                    else:
                        outward(k).wait()


def give(table, j, edges, arrivals, count):
    width = len(edges)
    spots = [(a, at) for a, array in enumerate(arrivals) for at in range(array.shape[0])][:count]
    arrivals = arrivals[: 1 + spots[-1][0]]
    anywhere = pl.BlockSpec(memory_space=pl.ANY)
    shape = (1,) + arrivals[0].shape[1:]
    given = pl.pallas_call(
        functools.partial(give_kernel, give_at + j * width, width, spots),
        out_shape=[jax.ShapeDtypeStruct(shape, arrivals[0].dtype)] * width,
        in_specs=[pl.BlockSpec(memory_space=pltpu.SMEM)] + [anywhere] * len(arrivals),
        out_specs=[anywhere] * width,
        scratch_shapes=[
            pltpu.VMEM((width,) + shape[1:], arrivals[0].dtype),
            pltpu.SemaphoreType.DMA((width,)),
            pltpu.SemaphoreType.DMA((width,)),
        ],
        compiler_params=pltpu.CompilerParams(vmem_limit_bytes=(4 + width) << 20),
        cost_estimate=pl.CostEstimate(flops=0, bytes_accessed=4096, transcendentals=0),
        name="give",
    )(table, *arrivals)
    return [lax.ppermute(a, ("groups", "batch"), routes(edge)) for a, edge in zip(given, edges)]


def project(tokens, q_weight, kv_weight, block_tokens, lengths, rank, n):
    parity = rank // (n // 2)
    row_count, steps, depth = tokens.shape
    widened = tokens.astype(jnp.float32)
    normed = (
        widened * lax.rsqrt(jnp.mean(widened * widened, axis=-1, keepdims=True) + eps_norm)
    ).astype(jnp.bfloat16)
    flattened = normed.reshape(row_count * steps, depth)
    query_part = jnp.dot(flattened, q_weight, preferred_element_type=jnp.float32).astype(jnp.bfloat16)
    pair_part = jnp.dot(flattened, kv_weight, preferred_element_type=jnp.float32).astype(jnp.bfloat16)
    query_part, pair_part = lax.optimization_barrier((query_part, pair_part))
    starts = (lengths.reshape(-1) * block_tokens).astype(jnp.float32)
    positions = starts[:, None] + jnp.arange(steps, dtype=jnp.float32)[None, :]

    def turned(rows):
        shaped = rows.astype(jnp.float32).reshape(row_count, steps, -1, HD)
        return rotate(shaped, positions).astype(jnp.bfloat16).reshape(rows.shape)

    queries = turned(query_part)
    pairs = jnp.where(parity == 0, turned(pair_part), pair_part)
    return queries, pairs


def head_routes(n):
    w = n // 2
    return [[(t, ((t + flip) % 2) * w + t // 2) for t in range(n)] for flip in range(2)]


def exchange(queries, pairs, lengths, rank, n):
    w = n // 2
    parity, core = rank // w, rank % 2
    per_group = lengths.shape[1]
    steps = queries.shape[0] // (2 * per_group)
    heads = KV // w
    ratio = QH // KV
    group_rows = per_group * steps

    def group_of(rows, which):
        return lax.dynamic_slice_in_dim(rows, which * group_rows, group_rows, 0)

    to_same, to_cross = head_routes(n)
    same = lax.ppermute(group_of(queries, core), "tensor", to_same)
    cross = lax.ppermute(group_of(queries, 1 - core), "tensor", to_cross)
    own_pair = group_of(pairs, parity)
    far_pair = lax.ppermute(
        group_of(pairs, 1 - parity), "tensor", [(t, (t + w) % n) for t in range(n)]
    )
    first = jnp.where(parity == 0, same, cross)
    second = jnp.where(parity == 0, cross, same)
    held = jnp.concatenate([first, second], axis=1).reshape(per_group, steps, heads, ratio, HD)
    held = jnp.transpose(held, (0, 2, 1, 3, 4)).reshape(per_group, heads * steps * ratio, HD)

    def fresh(rows):
        shaped = jnp.transpose(rows.reshape(per_group, steps, heads, HD), (0, 2, 1, 3))
        return jnp.pad(shaped, ((0, 0), (0, 0), (0, 16 - steps), (0, 0)))

    fresh_keys = fresh(jnp.where(parity == 0, own_pair, far_pair))
    fresh_values = fresh(jnp.where(parity == 0, far_pair, own_pair))
    return held, fresh_keys, fresh_values


def attention(held, fresh_keys, fresh_values, keys, values, lengths, steps, rank, n):
    parity, core = rank // (n // 2), rank % 2
    per_group, heads = fresh_keys.shape[:2]
    blocks = keys.shape[0]
    ratio = QH // KV
    group_rows = per_group * steps
    to_same, to_cross = head_routes(n)
    own_lengths = jnp.where(parity == 0, lengths[0], lengths[1])
    ends = jnp.cumsum(own_lengths)
    request_of = jnp.sum(
        (jnp.arange(blocks)[:, None] >= ends[None, :]).astype(jnp.int32), axis=1
    )
    out = attend(request_of, held, fresh_keys, fresh_values, keys, values, steps)
    out = jnp.transpose(out.reshape(per_group, heads, steps, ratio * HD), (0, 2, 1, 3))
    out = out.reshape(group_rows, heads * ratio * HD)
    width = heads * ratio * HD // 2
    lower, upper = out[:, :width], out[:, width:]
    back_same = lax.ppermute(
        jnp.where(parity == 0, lower, upper), "tensor", [(d, t) for t, d in to_same]
    )
    back_cross = lax.ppermute(
        jnp.where(parity == 0, upper, lower), "tensor", [(d, t) for t, d in to_cross]
    )
    groups = [jnp.where(core == 0, back_same, back_cross), jnp.where(core == 0, back_cross, back_same)]
    return jnp.concatenate(groups, axis=0).reshape(2 * per_group, steps, width)


early_sizes = (2, 2)
least_total = ahead + sum(early_sizes)
tie = lax.optimization_barrier


def routes(edge):
    return [(r, t) for r, t in enumerate(edge) if t >= 0]


def neighbours(groups, batch):
    across, beside = [], []
    for g in range(groups):
        for b in range(batch):
            across.append((g ^ 1) * batch + b if g ^ 1 < groups else -1)
            beside.append(g * batch + (b ^ 1) if b ^ 1 < batch else -1)
    return [across, beside]


def finish_two_chips(total, edges, operands):
    table, keys, values, home, head, arrived, early, ready = operands
    n = lax.axis_size("tensor")
    slot_count = 8 * keys.shape[0] // (3 * n)
    chip_pairs = [(t, (t + 2) % n) for t in range(n)]
    core_pairs = [(t, t ^ 1) for t in range(n)]
    width = len(edges)
    last = []
    for i in range(total - least_total):
        sent = ready[i]
        if i >= 2:
            sent, _ = tie((sent, last[i - 2]))
        last.append(lax.ppermute(sent, "tensor", chip_pairs))
    late = give(table, 1, edges, list(arrived) + last, total - ahead - 1)
    parts, low = [(place_at, head, None)], place_at + ahead
    for array in arrived:
        parts.append((low, array, None))
        low += array.shape[0]
    parts += [(back_at + k, a, None) for k, a in enumerate(early)]
    for i, array in enumerate(last):
        parts.append((low + i, array, last[min(i + 1, len(last) - 1)]))
    parts += [(back_at + width + k, a, None) for k, a in enumerate(late)]
    pools = place_home(table, (keys, values), home, slot_count)
    waiting = None
    for at, mine, following in parts:
        if following is not None:
            mine, pools, _ = tie((mine, pools, following))
        other = lax.ppermute(mine, "tensor", core_pairs)
        if waiting is not None:
            pools = place(table, *waiting, pools)
        waiting = (at, mine, other)
    return place(table, *waiting, pools)


def shared(own, row, rows):
    if rows & (rows - 1):
        return lax.all_gather(own, ("groups", "batch"))
    known, bit = own[None], 1
    while bit < rows:
        other = lax.ppermute(known, ("groups", "batch"), [(r, r ^ bit) for r in range(rows)])
        upper = (row & bit) > 0
        known = jnp.concatenate(
            [jnp.where(upper, other, known), jnp.where(upper, known, other)], axis=0
        )
        bit *= 2
    return known


def two_chips(tokens, q_weight, kv_weight, keys, values, lengths, block_owner, rank, n):
    chip_pairs = [(t, (t + 2) % n) for t in range(n)]
    core_pairs = [(t, t ^ 1) for t in range(n)]
    groups, batch = lax.axis_size("groups"), lax.axis_size("batch")
    row = lax.axis_index("groups") * batch + lax.axis_index("batch")
    edges = neighbours(groups, batch)
    width = len(edges)
    base = plan(block_owner, rank)
    home = [lax.ppermute(a, "tensor", core_pairs) for a in (keys, values)]
    (first,) = gather(base, own_at, (ahead,), (keys, values))
    handed = gather(base, lent_at, (lent,) * width, (keys, values))
    head = lax.ppermute(first, "tensor", chip_pairs)
    everyone = shared(block_owner, row, groups * batch)
    everyone, *handed = tie((everyone, *handed))
    borrowed = [
        lax.ppermute(a, ("groups", "batch"), routes(edge))
        for a, edge in zip(handed, edges)
    ]
    counts = jnp.sum(
        (everyone // 2 != jnp.arange(2)[None, :, None]).astype(jnp.int32), axis=2
    )
    flow, total = route(edges, counts)
    near = [jnp.array(edge, jnp.int32)[row] for edge in edges]
    places = jnp.stack([row, rank] + near).astype(jnp.int32)
    table = assign(width, least_total, flow, total, counts, base, places)
    tokens, table = tie((tokens, table))
    queries, pairs = project(tokens, q_weight, kv_weight, keys.shape[1], lengths, rank, n)
    queries, pairs, head, *home = tie((queries, pairs, head, *home))
    held = exchange(queries, pairs, lengths, rank, n)
    sent = pick(table, 0, early_sizes, (keys, values), borrowed)
    *sent, held = tie((*sent, held))
    arrived = [lax.ppermute(a, "tensor", chip_pairs) for a in sent]
    context = attention(*held, keys, values, lengths, tokens.shape[1], rank, n)
    rest = keys.shape[0] - least_total
    ready = pick(table, sum(early_sizes), (1,) * rest, (keys, values), borrowed)
    early = give(table, 0, edges, arrived[:1], width)
    totals = list(range(least_total, keys.shape[0] - 1)) + [keys.shape[0]]
    which = jnp.clip(total[0] - least_total, 0, len(totals) - 1)
    which, context = tie((which, context))
    operands = (table, keys, values, home, head, arrived, early, ready)
    new_keys, new_values = lax.switch(
        which,
        [functools.partial(finish_two_chips, count, edges) for count in totals],
        operands,
    )
    return context, new_keys, new_values


def move_padded(keys, values, block_owner, rank, n):
    parity = rank // (n // 2)
    blocks, block_tokens, width = keys.shape
    slot_count = 8 * blocks // (3 * n)
    own_owner = jnp.where(parity == 0, block_owner[0], block_owner[1])
    block_ids = jnp.arange(blocks)
    slot_ids = jnp.arange(slot_count)
    same_owner = own_owner[:, None] == own_owner[None, :]
    block_rank = jnp.sum(
        (same_owner & (block_ids[:, None] > block_ids[None, :])).astype(jnp.int32), axis=1
    )
    chosen = (own_owner[None, None, :] == jnp.arange(n)[None, :, None]) & (
        block_rank[None, None, :] == slot_ids[:, None, None]
    )
    selector = chosen.astype(jnp.bfloat16)
    counts = jnp.sum((block_owner == rank).astype(jnp.int32), axis=1)
    target = jnp.stack([slot_ids, counts[0] + slot_ids])
    filled = slot_ids[None, :] < counts[:, None]
    placement = ((target[None] == slot_ids[:, None, None]) & filled[None]).astype(jnp.bfloat16)
    moved = []
    for pool in (keys, values):
        send = jnp.einsum(
            "cdi,itl->cdtl", selector, pool, preferred_element_type=jnp.float32
        ).astype(jnp.bfloat16)
        got = lax.all_to_all(send, "tensor", split_axis=1, concat_axis=3, tiled=True)
        unpacked = got.reshape(slot_count, block_tokens, 2, KV * HD)
        moved.append(
            jnp.einsum(
                "spc,ctpl->stl", placement, unpacked, preferred_element_type=jnp.float32
            ).astype(jnp.bfloat16)
        )
    return moved


def per_device(tokens, q_weight, kv_weight, old_keys, old_values, lengths, block_owner):
    n = lax.axis_size("tensor")
    rank = lax.axis_index("tensor")
    keys, values = old_keys[0], old_values[0]
    if n == 4:
        context, new_keys, new_values = two_chips(
            tokens, q_weight, kv_weight, keys, values, lengths, block_owner, rank, n
        )
    else:
        new_keys, new_values = move_padded(keys, values, block_owner, rank, n)
        queries, pairs = project(tokens, q_weight, kv_weight, keys.shape[1], lengths, rank, n)
        held = exchange(queries, pairs, lengths, rank, n)
        context = attention(*held, keys, values, lengths, tokens.shape[1], rank, n)
    return (context, new_keys[None], new_values[None])


def solution(mesh):
    return jax.shard_map(
        per_device,
        mesh=mesh,
        in_specs=(
            P(("groups", "batch"), None, None),
            P(None, "tensor"),
            P(None, "tensor"),
            P("tensor", ("groups", "batch"), None, None),
            P("tensor", ("groups", "batch"), None, None),
            P(("groups", "batch"), None),
            P(("groups", "batch"), None),
        ),
        out_specs=(
            P(("groups", "batch"), None, "tensor"),
            P(("groups", "batch"), "tensor", None, None),
            P(("groups", "batch"), "tensor", None, None),
        ),
        check_vma=False,
    )
```

```python
import functools
import jax
import jax.numpy as jnp
from jax import lax
from jax.experimental import pallas as pl
from jax.experimental.pallas import tpu as pltpu
from jax.sharding import PartitionSpec as P

HD = 128
QH = 64
KV = 8
theta_base = 1000000.0
eps_norm = 1e-06
masked_low = -1e30


def rotate(vectors, positions):
    half_dim = vectors.shape[-1] // 2
    frequency = theta_base ** (-2.0 * jnp.arange(half_dim, dtype=jnp.float32) / vectors.shape[-1])
    angles = positions[..., None, None] * frequency
    cosine = jnp.cos(angles)
    sine_part = jnp.sin(angles)
    lower_half = vectors[..., :half_dim]
    upper_half = vectors[..., half_dim:]
    return jnp.concatenate(
        [
            lower_half * cosine - upper_half * sine_part,
            upper_half * cosine + lower_half * sine_part,
        ],
        axis=-1,
    )


def attend_kernel(steps, heads, request_ref, q_ref, fk_ref, fv_ref, k_ref, v_ref, out_ref, held, fresh, top, total, accum):
    step = pl.program_id(0)
    blocks = held.shape[0]
    requests = q_ref.shape[0]
    rows = q_ref.shape[1] // heads
    ratio = rows // steps
    scale = HD ** (-0.5)
    contract = (((1,), (1,)), ((), ()))

    @pl.when(step == 0)
    def _():
        padded = fk_ref.shape[2]
        row_step = lax.broadcasted_iota(jnp.int32, (rows, padded), 0) // ratio
        column = lax.broadcasted_iota(jnp.int32, (rows, padded), 1)
        causal = (column <= row_step) & (column < steps)
        for j in range(requests):
            for h in range(heads):
                part = pl.ds(h * rows, rows)
                scores = lax.dot_general(
                    q_ref[j, part, :], fk_ref[j, h], contract, preferred_element_type=jnp.float32
                )
                scores = jnp.where(causal, scores * scale, masked_low)
                fresh[j, part, :] = scores
                peak = jnp.max(scores, axis=-1, keepdims=True)
                top[j, part, :] = jnp.broadcast_to(peak, (rows, HD))

    @pl.when(step < blocks)
    def _():
        j = request_ref[step]
        for h in range(heads):
            part = pl.ds(h * rows, rows)
            scores = (
                lax.dot_general(
                    q_ref[j, part, :],
                    k_ref[0, :, pl.ds(h * HD, HD)],
                    contract,
                    preferred_element_type=jnp.float32,
                )
                * scale
            )
            held[step, part, :] = scores
            top[j, part, :] = jnp.maximum(
                top[j, part, :], jnp.max(scores, axis=-1, keepdims=True)
            )

    @pl.when(step == blocks)
    def _():
        for j in range(requests):
            for h in range(heads):
                part = pl.ds(h * rows, rows)
                probs = jnp.exp(fresh[j, part, :] - top[j, part, :1])
                total[j, part, :] = jnp.broadcast_to(
                    jnp.sum(probs, axis=-1, keepdims=True), (rows, HD)
                )
                accum[j, part, :] = jnp.dot(
                    probs.astype(jnp.bfloat16), fv_ref[j, h], preferred_element_type=jnp.float32
                )

    @pl.when(step >= blocks)
    def _():
        j = request_ref[step - blocks]
        for h in range(heads):
            part = pl.ds(h * rows, rows)
            probs = jnp.exp(held[step - blocks, part, :] - top[j, part, :1])
            total[j, part, :] += jnp.sum(probs, axis=-1, keepdims=True)
            accum[j, part, :] += jnp.dot(
                probs.astype(jnp.bfloat16),
                v_ref[0, :, pl.ds(h * HD, HD)],
                preferred_element_type=jnp.float32,
            )

    @pl.when(step == pl.num_programs(0) - 1)
    def _():
        out_ref[...] = (accum[...] / total[...]).astype(out_ref.dtype)


def attend(request_of, queries, fresh_keys, fresh_values, keys, values, steps):
    requests, heads = fresh_keys.shape[:2]
    blocks, tokens, width = keys.shape
    whole = lambda shape: pl.BlockSpec(shape, lambda i, r: (0,) * len(shape))
    state = pltpu.VMEM(queries.shape, jnp.float32)
    return pl.pallas_call(
        functools.partial(attend_kernel, steps, heads),
        out_shape=jax.ShapeDtypeStruct(queries.shape, jnp.bfloat16),
        grid_spec=pltpu.PrefetchScalarGridSpec(
            num_scalar_prefetch=1,
            grid=(2 * blocks,),
            in_specs=[
                whole(queries.shape),
                whole(fresh_keys.shape),
                whole(fresh_values.shape),
                pl.BlockSpec(
                    (1, tokens, width), lambda i, r: (jnp.minimum(i, blocks - 1), 0, 0)
                ),
                pl.BlockSpec(
                    (1, tokens, width), lambda i, r: (jnp.maximum(i - blocks, 0), 0, 0)
                ),
            ],
            out_specs=whole(queries.shape),
            scratch_shapes=[
                pltpu.VMEM((blocks, queries.shape[1], tokens), jnp.float32),
                pltpu.VMEM(queries.shape[:2] + fresh_keys.shape[2:3], jnp.float32),
                state,
                state,
                state,
            ],
        ),
        compiler_params=pltpu.CompilerParams(vmem_limit_bytes=32 * 1024 * 1024),
        cost_estimate=pl.CostEstimate(flops=0, bytes_accessed=4096, transcendentals=0),
        name="attend",
    )(request_of, queries, fresh_keys, fresh_values, keys, values)


def settle(table, offset, count, arrivals, outs, buffers, sem):
    mine, other = arrivals
    width = mine[0].shape[-1]

    def inward(i, side):
        places = pl.ds(side * width, width), pl.ds((1 - side) * width, width)
        return [
            pltpu.make_async_copy(half[a].at[i], buffers[a].at[i, :, place], sem.at[i, 2 * a + s])
            for a in range(2)
            for s, (half, place) in enumerate(zip((mine, other), places))
        ]

    def outward(i):
        slot = table[offset + i]
        return [
            pltpu.make_async_copy(buffers[a].at[i], outs[a].at[slot], sem.at[i, 4 + a])
            for a in range(2)
        ]

    for side in range(2):

        @pl.when(table[core_at] == side)
        def _():
            for i in range(count):

                @pl.when(table[offset + i] >= 0)
                def _():
                    for copy in inward(i, side):
                        copy.start()

            for i in range(count):

                @pl.when(table[offset + i] >= 0)
                def _():
                    for copy in inward(i, side):
                        copy.wait()
                    for copy in outward(i):
                        copy.start()

            for i in range(count):

                @pl.when(table[offset + i] >= 0)
                def _():
                    for copy in outward(i):
                        copy.wait()


def place_kernel(offset, count, table, mine, other, kin_ref, vin_ref, k_out, v_out, kbuf, vbuf, sem):
    del kin_ref, vin_ref
    halves = [[ref.at[:, a] for a in range(2)] for ref in (mine, other)]
    settle(table, offset, count, halves, (k_out, v_out), (kbuf, vbuf), sem)


def place(table, offset, mine, other, pools):
    count = mine.shape[0]
    anywhere = pl.BlockSpec(memory_space=pl.ANY)
    buffer = pltpu.VMEM((count,) + pools[0].shape[1:], pools[0].dtype)
    return pl.pallas_call(
        functools.partial(place_kernel, offset, count),
        out_shape=[jax.ShapeDtypeStruct(a.shape, a.dtype) for a in pools],
        in_specs=[pl.BlockSpec(memory_space=pltpu.SMEM)] + [anywhere] * 4,
        out_specs=[anywhere] * 2,
        scratch_shapes=[buffer, buffer, pltpu.SemaphoreType.DMA((count, 6))],
        input_output_aliases={3: 0, 4: 1},
        compiler_params=pltpu.CompilerParams(vmem_limit_bytes=(4 + 2 * count) << 20),
        cost_estimate=pl.CostEstimate(flops=0, bytes_accessed=4096, transcendentals=0),
        name="place",
    )(table, mine, other, *pools)


def home_kernel(table, km_ref, vm_ref, ko_ref, vo_ref, k_out, v_out, kbuf, vbuf, blank, sem, blank_sem):
    slots = k_out.shape[0]
    blank[...] = jnp.zeros_like(blank)

    def clearing(i):
        return [
            pltpu.make_async_copy(blank, out.at[i], blank_sem.at[i, a])
            for a, out in enumerate((k_out, v_out))
        ]

    for i in range(slots):

        @pl.when(i >= table[filled_at])
        def _():
            for copy in clearing(i):
                copy.start()

    halves = ((km_ref, vm_ref), (ko_ref, vo_ref))
    settle(table, home_at, km_ref.shape[0], halves, (k_out, v_out), (kbuf, vbuf), sem)
    for i in range(slots):

        @pl.when(i >= table[filled_at])
        def _():
            for copy in clearing(i):
                copy.wait()


def place_home(table, mine, other, slot_count):
    blocks, block_tokens, width = mine[0].shape
    anywhere = pl.BlockSpec(memory_space=pl.ANY)
    buffer = pltpu.VMEM((blocks, block_tokens, 2 * width), mine[0].dtype)
    pool = jax.ShapeDtypeStruct((slot_count, block_tokens, 2 * width), mine[0].dtype)
    return pl.pallas_call(
        home_kernel,
        out_shape=[pool, pool],
        in_specs=[pl.BlockSpec(memory_space=pltpu.SMEM)] + [anywhere] * 4,
        out_specs=[anywhere] * 2,
        scratch_shapes=[
            buffer,
            buffer,
            pltpu.VMEM((block_tokens, 2 * width), mine[0].dtype),
            pltpu.SemaphoreType.DMA((blocks, 6)),
            pltpu.SemaphoreType.DMA((slot_count, 2)),
        ],
        compiler_params=pltpu.CompilerParams(vmem_limit_bytes=(6 + 2 * blocks) << 20),
        cost_estimate=pl.CostEstimate(flops=0, bytes_accessed=4096, transcendentals=0),
        name="place_home",
    )(table, *mine, *other)


own_at, home_at, far_at, core_at, filled_at, lent_at = 0, 16, 32, 48, 49, 52
pick_at, place_at, give_at, back_at, table_size = 64, 80, 96, 104, 128
lent = 2
ahead = 3


def plan_kernel(owner_ref, rank_ref, table):
    rank = rank_ref[0]
    parity = rank // 2
    for i in range(table.shape[0]):
        table[i] = 0
    for i in range(far_at, core_at):
        table[i] = -1
    slot, leaving, coming = jnp.int32(0), jnp.int32(0), jnp.int32(0)
    for p in range(2):
        own = (parity == p).astype(jnp.int32)
        for i in range(owner_ref.shape[1]):
            owner = owner_ref[p, i]
            mine = owner == rank
            value = jnp.where(mine, slot, -1)
            slot = slot + mine.astype(jnp.int32)
            crossing = (owner // 2 != p).astype(jnp.int32)

            @pl.when(own == 1)
            def _():
                table[home_at + i] = value

            @pl.when(own * crossing == 1)
            def _():
                table[own_at + leaving] = i

            @pl.when((1 - own) * crossing == 1)
            def _():
                table[far_at + coming] = value

            leaving = leaving + own * crossing
            coming = coming + (1 - own) * crossing
    table[core_at] = rank % 2
    table[filled_at] = slot
    for i in range(lent_at, pick_at):
        table[i] = table[own_at + jnp.maximum(leaving - 1 - (i - lent_at), 0)]


def plan(block_owner, rank):
    scalars = pl.BlockSpec(memory_space=pltpu.SMEM)
    return pl.pallas_call(
        plan_kernel,
        out_shape=jax.ShapeDtypeStruct((64,), jnp.int32),
        in_specs=[scalars, scalars],
        out_specs=scalars,
        name="plan",
    )(block_owner, rank[None].astype(jnp.int32))


def gather_kernel(starts, table, k_ref, v_ref, *outs):
    for start, end, out in zip(starts[:-1], starts[1:], outs):

        @pl.when((pl.program_id(0) >= start) & (pl.program_id(0) < end))
        def _():
            out[0, 0] = k_ref[0]
            out[0, 1] = v_ref[0]


def gather(table, offset, sizes, sources):
    count = sum(sizes)
    shape = (1,) + sources[0].shape[1:]
    taken = pl.BlockSpec(shape, lambda i, table: (table[offset + i], 0, 0))
    starts = [sum(sizes[:i]) for i in range(len(sizes) + 1)]
    return pl.pallas_call(
        functools.partial(gather_kernel, starts),
        out_shape=[
            jax.ShapeDtypeStruct((size, 2) + shape[1:], sources[0].dtype) for size in sizes
        ],
        grid_spec=pltpu.PrefetchScalarGridSpec(
            num_scalar_prefetch=1,
            grid=(count,),
            in_specs=[taken, taken],
            out_specs=[
                pl.BlockSpec(
                    (1, 2) + shape[1:],
                    lambda i, table, size=size, start=start: (
                        jnp.clip(i - start, 0, size - 1),
                        0,
                        0,
                        0,
                    ),
                )
                for size, start in zip(sizes, starts)
            ],
        ),
        cost_estimate=pl.CostEstimate(flops=0, bytes_accessed=4096, transcendentals=0),
        compiler_params=pltpu.CompilerParams(vmem_limit_bytes=40 << 20),
        name="gather",
    )(table, *sources)


def route_kernel(edges, count_ref, flow_out, total_out):
    rows = count_ref.shape[0]
    lane = lax.broadcasted_iota(jnp.int32, (1, 128), 1)
    total, direction = lane & 15, lane >> 4
    counts = [jnp.where(direction == 0, count_ref[r, 0], count_ref[r, 1]) for r in range(rows)]
    excess = [jnp.maximum(c - total, 0) for c in counts]
    free = [jnp.maximum(total - jnp.maximum(c, ahead + 1), 0) for c in counts]
    width = len(edges)
    flow = [[jnp.zeros((1, 128), jnp.int32) for _ in range(width)] for _ in range(rows)]
    limit = [
        [jnp.clip(c - ahead - lent * k, 0, lent) for k in range(width)] for c in counts
    ]
    for _ in range(lent * width):
        for r in range(rows):
            marks = []
            for k, edge in enumerate(edges):
                near = edge[r]
                if near < 0:
                    marks.append(jnp.zeros((1, 128), jnp.int32))
                    continue
                can = (flow[r][k] < limit[r][k]) & (free[near] > 0) & (excess[r] > 0)
                marks.append(jnp.where(can, free[near] * 4 + 3 - k, 0))
            best = functools.reduce(jnp.maximum, marks)
            for k, edge in enumerate(edges):
                near = edge[r]
                if near >= 0:
                    took = jnp.where((marks[k] == best) & (best > 0), 1, 0)
                    flow[r][k] = flow[r][k] + took
                    free[near] = free[near] - took
                    excess[r] = excess[r] - took
    left = functools.reduce(jnp.maximum, excess)
    wrong = (left > 0) & (direction < 2) & (total <= 12)
    total_out[0] = jnp.max(jnp.where(wrong, total, 0)) + 1
    flow_out[...] = jnp.zeros_like(flow_out)
    for r in range(rows):
        for k in range(width):
            flow_out[pl.ds(r * width + k, 1), :] = flow[r][k]


def route(edges, counts):
    rows = counts.shape[0]
    height = -(-rows * len(edges) // 8) * 8
    return pl.pallas_call(
        functools.partial(route_kernel, edges),
        out_shape=[
            jax.ShapeDtypeStruct((height, 128), jnp.int32),
            jax.ShapeDtypeStruct((1,), jnp.int32),
        ],
        in_specs=[pl.BlockSpec(memory_space=pltpu.SMEM)],
        out_specs=[
            pl.BlockSpec(memory_space=pltpu.VMEM),
            pl.BlockSpec(memory_space=pltpu.SMEM),
        ],
        name="route",
    )(counts)


def assign_kernel(width, least, flow_ref, total_ref, count_ref, base_ref, place_ref, table):
    row, rank = place_ref[0], place_ref[1]
    parity = rank // 2
    total = jnp.maximum(total_ref[0], least)
    for i in range(pick_at):
        table[i] = base_ref[i]
    for i in range(pick_at, place_at):
        table[i] = 0
    for i in range(place_at, table_size):
        table[i] = -1
    for side in range(2):
        direction = parity if side == 0 else 1 - parity
        lane = total + 16 * direction
        count = count_ref[row, direction]
        slot = jnp.int32(0)
        for j in range(lent):
            for k in range(width):
                near = place_ref[2 + k]
                helped = (near >= 0) & (flow_ref[jnp.maximum(near, 0) * width + k, lane] > j)

                @pl.when(helped)
                def _():
                    if side == 0:
                        table[pick_at + slot] = 64 * (k + 1) + j
                    else:
                        table[give_at + j * width + k] = slot

                slot = slot + helped.astype(jnp.int32)
        blocks = home_at - 4
        for position in range(blocks):
            after = jnp.maximum(count - 1 - position, 0)
            k, j = after // lent, after % lent
            handed = (k < width) & (flow_ref[row * width + jnp.minimum(k, width - 1), lane] > j)
            held = position < count
            direct = held & jnp.logical_not(handed) & (position >= ahead)

            @pl.when(direct)
            def _():
                if side == 0:
                    table[pick_at + slot] = base_ref[own_at + position]
                else:
                    table[place_at + ahead + slot] = base_ref[far_at + position]

            if side == 1:

                @pl.when(held & handed)
                def _():
                    table[back_at + j * width + k] = base_ref[far_at + position]

                if position < ahead:

                    @pl.when(held)
                    def _():
                        table[place_at + position] = base_ref[far_at + position]

            slot = slot + direct.astype(jnp.int32)


def assign(width, least, flow, total, counts, base, places):
    scalars = pl.BlockSpec(memory_space=pltpu.SMEM)
    return pl.pallas_call(
        functools.partial(assign_kernel, width, least),
        out_shape=jax.ShapeDtypeStruct((table_size,), jnp.int32),
        in_specs=[scalars] * 5,
        out_specs=scalars,
        name="assign",
    )(flow, total, counts, base, places)


def pick_kernel(offset, sizes, sources, table, k_ref, v_ref, *rest):
    lent_refs, outs = rest[:sources], rest[sources : sources + len(sizes)]
    buffer, sem, out_sem = rest[sources + len(sizes) :]
    spots = [(out, at) for out, size in zip(outs, sizes) for at in range(size)]

    def inward(i, kind):
        index = table[pick_at + offset + i] & 63
        if kind == 0:
            pair = k_ref.at[index], v_ref.at[index]
        else:
            pair = lent_refs[kind - 1].at[index, 0], lent_refs[kind - 1].at[index, 1]
        return [pltpu.make_async_copy(pair[a], buffer.at[i, a], sem.at[i, a]) for a in range(2)]

    def outward(i):
        out, at = spots[i]
        return pltpu.make_async_copy(buffer.at[i], out.at[at], out_sem.at[i])

    for phase in range(2):
        for i in range(len(spots)):
            for kind in range(sources + 1):

                @pl.when(table[pick_at + offset + i] >> 6 == kind)
                def _():
                    for copy in inward(i, kind):
                        if phase == 0:
                            copy.start()
                        else:
                            copy.wait()

            if phase == 1:
                outward(i).start()
    for i in range(len(spots)):
        outward(i).wait()


def pick(table, offset, sizes, own, borrowed):
    scalars = pl.BlockSpec(memory_space=pltpu.SMEM)
    anywhere = pl.BlockSpec(memory_space=pl.ANY)
    count = sum(sizes)
    shape = (2,) + own[0].shape[1:]
    return pl.pallas_call(
        functools.partial(pick_kernel, offset, sizes, len(borrowed)),
        out_shape=[jax.ShapeDtypeStruct((size,) + shape, own[0].dtype) for size in sizes],
        in_specs=[scalars] + [anywhere] * (2 + len(borrowed)),
        out_specs=[anywhere] * len(sizes),
        scratch_shapes=[
            pltpu.VMEM((count,) + shape, own[0].dtype),
            pltpu.SemaphoreType.DMA((count, 2)),
            pltpu.SemaphoreType.DMA((count,)),
        ],
        compiler_params=pltpu.CompilerParams(vmem_limit_bytes=(4 + count) << 20),
        cost_estimate=pl.CostEstimate(flops=0, bytes_accessed=4096, transcendentals=0),
        name="pick",
    )(table, *own, *borrowed)


def give_kernel(offset, width, spots, table, *rest):
    many = 1 + max(array for array, _ in spots)
    arrivals, outs = rest[:many], rest[many : many + width]
    buffer, sem, out_sem = rest[many + width :]

    def inward(k, choice):
        array, at = spots[choice]
        return pltpu.make_async_copy(arrivals[array].at[at], buffer.at[k], sem.at[k])

    def outward(k):
        return pltpu.make_async_copy(buffer.at[k], outs[k].at[0], out_sem.at[k])

    for phase in range(3):
        for k in range(width):
            for choice in range(len(spots)):

                @pl.when(table[offset + k] == choice)
                def _():
                    if phase == 0:
                        inward(k, choice).start()
                    elif phase == 1:
                        inward(k, choice).wait()
                        outward(k).start()
                    else:
                        outward(k).wait()


def give(table, j, edges, arrivals, count):
    width = len(edges)
    spots = [(a, at) for a, array in enumerate(arrivals) for at in range(array.shape[0])][:count]
    arrivals = arrivals[: 1 + spots[-1][0]]
    anywhere = pl.BlockSpec(memory_space=pl.ANY)
    shape = (1,) + arrivals[0].shape[1:]
    given = pl.pallas_call(
        functools.partial(give_kernel, give_at + j * width, width, spots),
        out_shape=[jax.ShapeDtypeStruct(shape, arrivals[0].dtype)] * width,
        in_specs=[pl.BlockSpec(memory_space=pltpu.SMEM)] + [anywhere] * len(arrivals),
        out_specs=[anywhere] * width,
        scratch_shapes=[
            pltpu.VMEM((width,) + shape[1:], arrivals[0].dtype),
            pltpu.SemaphoreType.DMA((width,)),
            pltpu.SemaphoreType.DMA((width,)),
        ],
        compiler_params=pltpu.CompilerParams(vmem_limit_bytes=(4 + width) << 20),
        cost_estimate=pl.CostEstimate(flops=0, bytes_accessed=4096, transcendentals=0),
        name="give",
    )(table, *arrivals)
    return [lax.ppermute(a, ("groups", "batch"), routes(edge)) for a, edge in zip(given, edges)]


def project(tokens, q_weight, kv_weight, block_tokens, lengths, rank, n):
    parity = rank // (n // 2)
    row_count, steps, depth = tokens.shape
    widened = tokens.astype(jnp.float32)
    normed = (
        widened * lax.rsqrt(jnp.mean(widened * widened, axis=-1, keepdims=True) + eps_norm)
    ).astype(jnp.bfloat16)
    flattened = normed.reshape(row_count * steps, depth)
    query_part = jnp.dot(flattened, q_weight, preferred_element_type=jnp.float32).astype(jnp.bfloat16)
    pair_part = jnp.dot(flattened, kv_weight, preferred_element_type=jnp.float32).astype(jnp.bfloat16)
    query_part, pair_part = lax.optimization_barrier((query_part, pair_part))
    starts = (lengths.reshape(-1) * block_tokens).astype(jnp.float32)
    positions = starts[:, None] + jnp.arange(steps, dtype=jnp.float32)[None, :]

    def turned(rows):
        shaped = rows.astype(jnp.float32).reshape(row_count, steps, -1, HD)
        return rotate(shaped, positions).astype(jnp.bfloat16).reshape(rows.shape)

    queries = turned(query_part)
    pairs = jnp.where(parity == 0, turned(pair_part), pair_part)
    return queries, pairs


def head_routes(n):
    w = n // 2
    return [[(t, ((t + flip) % 2) * w + t // 2) for t in range(n)] for flip in range(2)]


def exchange(queries, pairs, lengths, rank, n):
    w = n // 2
    parity, core = rank // w, rank % 2
    per_group = lengths.shape[1]
    steps = queries.shape[0] // (2 * per_group)
    heads = KV // w
    ratio = QH // KV
    group_rows = per_group * steps

    def group_of(rows, which):
        return lax.dynamic_slice_in_dim(rows, which * group_rows, group_rows, 0)

    to_same, to_cross = head_routes(n)
    same = lax.ppermute(group_of(queries, core), "tensor", to_same)
    cross = lax.ppermute(group_of(queries, 1 - core), "tensor", to_cross)
    own_pair = group_of(pairs, parity)
    far_pair = lax.ppermute(
        group_of(pairs, 1 - parity), "tensor", [(t, (t + w) % n) for t in range(n)]
    )
    first = jnp.where(parity == 0, same, cross)
    second = jnp.where(parity == 0, cross, same)
    held = jnp.concatenate([first, second], axis=1).reshape(per_group, steps, heads, ratio, HD)
    held = jnp.transpose(held, (0, 2, 1, 3, 4)).reshape(per_group, heads * steps * ratio, HD)

    def fresh(rows):
        shaped = jnp.transpose(rows.reshape(per_group, steps, heads, HD), (0, 2, 1, 3))
        return jnp.pad(shaped, ((0, 0), (0, 0), (0, 16 - steps), (0, 0)))

    fresh_keys = fresh(jnp.where(parity == 0, own_pair, far_pair))
    fresh_values = fresh(jnp.where(parity == 0, far_pair, own_pair))
    return held, fresh_keys, fresh_values


def attention(held, fresh_keys, fresh_values, keys, values, lengths, steps, rank, n):
    parity, core = rank // (n // 2), rank % 2
    per_group, heads = fresh_keys.shape[:2]
    blocks = keys.shape[0]
    ratio = QH // KV
    group_rows = per_group * steps
    to_same, to_cross = head_routes(n)
    own_lengths = jnp.where(parity == 0, lengths[0], lengths[1])
    ends = jnp.cumsum(own_lengths)
    request_of = jnp.sum(
        (jnp.arange(blocks)[:, None] >= ends[None, :]).astype(jnp.int32), axis=1
    )
    out = attend(request_of, held, fresh_keys, fresh_values, keys, values, steps)
    out = jnp.transpose(out.reshape(per_group, heads, steps, ratio * HD), (0, 2, 1, 3))
    out = out.reshape(group_rows, heads * ratio * HD)
    width = heads * ratio * HD // 2
    lower, upper = out[:, :width], out[:, width:]
    back_same = lax.ppermute(
        jnp.where(parity == 0, lower, upper), "tensor", [(d, t) for t, d in to_same]
    )
    back_cross = lax.ppermute(
        jnp.where(parity == 0, upper, lower), "tensor", [(d, t) for t, d in to_cross]
    )
    groups = [jnp.where(core == 0, back_same, back_cross), jnp.where(core == 0, back_cross, back_same)]
    return jnp.concatenate(groups, axis=0).reshape(2 * per_group, steps, width)


early_sizes = (2, 2)
least_total = ahead + sum(early_sizes)
tie = lax.optimization_barrier


def routes(edge):
    return [(r, t) for r, t in enumerate(edge) if t >= 0]


def neighbours(groups, batch):
    across, beside = [], []
    for g in range(groups):
        for b in range(batch):
            across.append((g ^ 1) * batch + b if g ^ 1 < groups else -1)
            beside.append(g * batch + (b ^ 1) if b ^ 1 < batch else -1)
    return [across, beside]


def finish_two_chips(total, edges, operands):
    table, keys, values, home, head, arrived, early, ready = operands
    n = lax.axis_size("tensor")
    slot_count = 8 * keys.shape[0] // (3 * n)
    chip_pairs = [(t, (t + 2) % n) for t in range(n)]
    core_pairs = [(t, t ^ 1) for t in range(n)]
    width = len(edges)
    last = []
    for i in range(total - least_total):
        sent = ready[i]
        if i >= 2:
            sent, _ = tie((sent, last[i - 2]))
        last.append(lax.ppermute(sent, "tensor", chip_pairs))
    late = give(table, 1, edges, list(arrived) + last, total - ahead - 1)
    parts, low = [(place_at, head, None)], place_at + ahead
    for array in arrived:
        parts.append((low, array, None))
        low += array.shape[0]
    parts += [(back_at + k, a, None) for k, a in enumerate(early)]
    for i, array in enumerate(last):
        parts.append((low + i, array, last[min(i + 1, len(last) - 1)]))
    parts += [(back_at + width + k, a, None) for k, a in enumerate(late)]
    pools = place_home(table, (keys, values), home, slot_count)
    waiting = None
    for at, mine, following in parts:
        if following is not None:
            mine, pools, _ = tie((mine, pools, following))
        elif total <= least_total + 1 and at >= back_at + width:
            mine, pools, _ = tie((mine, pools, late))
        other = lax.ppermute(mine, "tensor", core_pairs)
        if waiting is not None:
            pools = place(table, *waiting, pools)
        waiting = (at, mine, other)
    return place(table, *waiting, pools)


def shared(own, row, rows):
    if rows & (rows - 1):
        return lax.all_gather(own, ("groups", "batch"))
    known, bit = own[None], 1
    while bit < rows:
        other = lax.ppermute(known, ("groups", "batch"), [(r, r ^ bit) for r in range(rows)])
        upper = (row & bit) > 0
        known = jnp.concatenate(
            [jnp.where(upper, other, known), jnp.where(upper, known, other)], axis=0
        )
        bit *= 2
    return known


def two_chips(tokens, q_weight, kv_weight, keys, values, lengths, block_owner, rank, n):
    chip_pairs = [(t, (t + 2) % n) for t in range(n)]
    core_pairs = [(t, t ^ 1) for t in range(n)]
    groups, batch = lax.axis_size("groups"), lax.axis_size("batch")
    row = lax.axis_index("groups") * batch + lax.axis_index("batch")
    edges = neighbours(groups, batch)
    width = len(edges)
    base = plan(block_owner, rank)
    home = [lax.ppermute(a, "tensor", core_pairs) for a in (keys, values)]
    (first,) = gather(base, own_at, (ahead,), (keys, values))
    handed = gather(base, lent_at, (lent,) * width, (keys, values))
    head = lax.ppermute(first, "tensor", chip_pairs)
    everyone = shared(block_owner, row, groups * batch)
    everyone, *handed = tie((everyone, *handed))
    borrowed = [
        lax.ppermute(a, ("groups", "batch"), routes(edge))
        for a, edge in zip(handed, edges)
    ]
    counts = jnp.sum(
        (everyone // 2 != jnp.arange(2)[None, :, None]).astype(jnp.int32), axis=2
    )
    flow, total = route(edges, counts)
    near = [jnp.array(edge, jnp.int32)[row] for edge in edges]
    places = jnp.stack([row, rank] + near).astype(jnp.int32)
    table = assign(width, least_total, flow, total, counts, base, places)
    tokens, table = tie((tokens, table))
    queries, pairs = project(tokens, q_weight, kv_weight, keys.shape[1], lengths, rank, n)
    queries, pairs, head, *home = tie((queries, pairs, head, *home))
    held = exchange(queries, pairs, lengths, rank, n)
    sent = pick(table, 0, early_sizes, (keys, values), borrowed)
    *sent, held = tie((*sent, held))
    arrived = [lax.ppermute(a, "tensor", chip_pairs) for a in sent]
    context = attention(*held, keys, values, lengths, tokens.shape[1], rank, n)
    rest = keys.shape[0] - least_total
    ready = pick(table, sum(early_sizes), (1,) * rest, (keys, values), borrowed)
    early = give(table, 0, edges, arrived[:1], width)
    totals = list(range(least_total, keys.shape[0] - 1)) + [keys.shape[0]]
    which = jnp.clip(total[0] - least_total, 0, len(totals) - 1)
    which, context = tie((which, context))
    operands = (table, keys, values, home, head, arrived, early, ready)
    new_keys, new_values = lax.switch(
        which,
        [functools.partial(finish_two_chips, count, edges) for count in totals],
        operands,
    )
    return context, new_keys, new_values


def move_padded(keys, values, block_owner, rank, n):
    parity = rank // (n // 2)
    blocks, block_tokens, width = keys.shape
    slot_count = 8 * blocks // (3 * n)
    own_owner = jnp.where(parity == 0, block_owner[0], block_owner[1])
    block_ids = jnp.arange(blocks)
    slot_ids = jnp.arange(slot_count)
    same_owner = own_owner[:, None] == own_owner[None, :]
    block_rank = jnp.sum(
        (same_owner & (block_ids[:, None] > block_ids[None, :])).astype(jnp.int32), axis=1
    )
    chosen = (own_owner[None, None, :] == jnp.arange(n)[None, :, None]) & (
        block_rank[None, None, :] == slot_ids[:, None, None]
    )
    selector = chosen.astype(jnp.bfloat16)
    counts = jnp.sum((block_owner == rank).astype(jnp.int32), axis=1)
    target = jnp.stack([slot_ids, counts[0] + slot_ids])
    filled = slot_ids[None, :] < counts[:, None]
    placement = ((target[None] == slot_ids[:, None, None]) & filled[None]).astype(jnp.bfloat16)
    moved = []
    for pool in (keys, values):
        send = jnp.einsum(
            "cdi,itl->cdtl", selector, pool, preferred_element_type=jnp.float32
        ).astype(jnp.bfloat16)
        got = lax.all_to_all(send, "tensor", split_axis=1, concat_axis=3, tiled=True)
        unpacked = got.reshape(slot_count, block_tokens, 2, KV * HD)
        moved.append(
            jnp.einsum(
                "spc,ctpl->stl", placement, unpacked, preferred_element_type=jnp.float32
            ).astype(jnp.bfloat16)
        )
    return moved


def per_device(tokens, q_weight, kv_weight, old_keys, old_values, lengths, block_owner):
    n = lax.axis_size("tensor")
    rank = lax.axis_index("tensor")
    keys, values = old_keys[0], old_values[0]
    if n == 4:
        context, new_keys, new_values = two_chips(
            tokens, q_weight, kv_weight, keys, values, lengths, block_owner, rank, n
        )
    else:
        new_keys, new_values = move_padded(keys, values, block_owner, rank, n)
        queries, pairs = project(tokens, q_weight, kv_weight, keys.shape[1], lengths, rank, n)
        held = exchange(queries, pairs, lengths, rank, n)
        context = attention(*held, keys, values, lengths, tokens.shape[1], rank, n)
    return (context, new_keys[None], new_values[None])


def solution(mesh):
    return jax.shard_map(
        per_device,
        mesh=mesh,
        in_specs=(
            P(("groups", "batch"), None, None),
            P(None, "tensor"),
            P(None, "tensor"),
            P("tensor", ("groups", "batch"), None, None),
            P("tensor", ("groups", "batch"), None, None),
            P(("groups", "batch"), None),
            P(("groups", "batch"), None),
        ),
        out_specs=(
            P(("groups", "batch"), None, "tensor"),
            P(("groups", "batch"), "tensor", None, None),
            P(("groups", "batch"), "tensor", None, None),
        ),
        check_vma=False,
    )
```
